128 devices in a mesh: dp: 16 (over x_hi, z, core), seq: 8 (over y, x_lo).
Axes of the slice: x: 4 (x_hi: 2, x_lo: 2; x = x_hi * 2 + x_lo), y: 4, z: 4, core: 2. Of those that a mesh axis runs over, the one named last changes fastest.
Arguments:
- queries: bfloat16 [16384, 8192], P(('seq', 'dp')), may hold values from -4.5 to 4.5
- key_head_rows: bfloat16 [16384, 1024], P(('seq', 'dp')), may hold values from -4.5 to 4.5
- value_head_rows: bfloat16 [16384, 1024], P(('seq', 'dp')), may hold values from -6 to 6
- out_cotangent: bfloat16 [16384, 8192], P(('seq', 'dp')), may hold values from -6 to 6
- value_readout: bfloat16 [8192], replicated, may hold values from -0.29882812 to 0.29882812
- rewards: float32 [16384], P(('seq', 'dp')), may hold values from -1.5 to 1.5
- saved_values: float32 [16384], P(('seq', 'dp')), may hold values from -6 to 6
- episode_ends: int32 [16384], P(('seq', 'dp')), may hold values from 0 to 1, as said below
- segment_ids: int32 [16384], P(('seq', 'dp')), may hold values from 0 to 16, as said below
Outputs:
- query_grad: bfloat16 [16384, 8192], P(('seq', 'dp'))
- key_gradient: bfloat16 [16384, 1024], P(('seq', 'dp'))
- value_gradient: bfloat16 [16384, 1024], P(('seq', 'dp'))
- advantages: float32 [16384], P(('seq', 'dp'))
The draws below stay inside these ranges and needn't reach their ends.
Inputs may be any that keep to these rules, and one draw needn't show every extreme that they name: `episode_ends`: 1 marks the last token of an episode; each aligned block of 1024 tokens holds exactly one 1, never at the block's last token. `segment_ids`: the number of episode ends before the token in the whole array; it never falls and rises by one right after each end.
All inputs are finite; a program needn't handle non-finite values.
Results may differ from the reference program's by a relative error of at most 0.0059.
Values may be sent and summed in bfloat16 or wider, within the bound.
A program may use at most 192 MiB of HBM per device.

```python
import math
import jax
import jax.numpy as jnp
from jax import lax

QUERY_HEADS = 64
KEY_VALUE_HEADS = 8
HEAD_WIDTH = 128
TOK_DEV = 128
WINDOW_LENGTH = 2048
TOKEN_COUNT = 16384


def shared_ends(key):
    block_len = TOK_DEV * 8
    block_count = TOKEN_COUNT // block_len
    spots = jax.random.randint(key, (block_count,), 0, block_len - 1)
    position = jnp.arange(TOKEN_COUNT)
    block_of = position // block_len
    inside = position % block_len
    chosen = jnp.take(spots, block_of)
    return (inside == chosen).astype(jnp.int32)


def draw_episode_ends(key, part):
    return shared_ends(key)


def draw_segment_ids(key, part):
    end_flags = shared_ends(key)
    return (jnp.cumsum(end_flags) - end_flags).astype(jnp.int32)


def draw_queries(key, part):
    key = jax.random.fold_in(key, 11)
    entry_list = jnp.clip(jax.random.normal(key, (TOKEN_COUNT, QUERY_HEADS * HEAD_WIDTH), jnp.float32), -4.5, 4.5)
    return entry_list.astype(jnp.bfloat16)


def draw_key_head_rows(key, part):
    key = jax.random.fold_in(key, 13)
    entry_list = jnp.clip(jax.random.normal(key, (TOKEN_COUNT, KEY_VALUE_HEADS * HEAD_WIDTH), jnp.float32), -4.5, 4.5)
    return entry_list.astype(jnp.bfloat16)


def levels(own_key, extent, shards, smallest, largest):
    level, own = 1.0, jax.random.fold_in(own_key, 6)
    for dim, parts in shards:
        steps = jnp.exp(jax.random.uniform(jax.random.fold_in(own, dim), (parts,), jnp.float32, smallest / len(shards), largest / len(shards)))
        level = level * jnp.repeat(steps, extent[dim] // parts).reshape([-1 if axis == dim else 1 for axis in range(len(extent))])
    return level


def centred(stream_key, extent, width, most, cuts=(), kind=jnp.bfloat16):
    values = width * jax.random.normal(stream_key, extent, jnp.float32)
    if cuts:
        values = values * levels(stream_key, extent, cuts, -0.22, 0.18)
    return jnp.clip(values, -most, most).astype(kind)


def setup_inputs(seed: int = 0) -> dict:
    arg_keys = jax.random.split(jax.random.key(seed), 10)
    queries = draw_queries(jax.random.fold_in(arg_keys[9], 71), 0)
    key_head_rows = draw_key_head_rows(jax.random.fold_in(arg_keys[9], 71), 0)
    value_head_rows = centred(arg_keys[2], (TOKEN_COUNT, KEY_VALUE_HEADS * HEAD_WIDTH), 1.0, 6.0, ((0, 128),))
    out_cotangent = centred(arg_keys[3], (TOKEN_COUNT, QUERY_HEADS * HEAD_WIDTH), 1.0, 6.0, ((0, 128),))
    value_readout = centred(arg_keys[4], (QUERY_HEADS * HEAD_WIDTH,), 0.05, 0.29882812)
    rewards = centred(arg_keys[5], (TOKEN_COUNT,), (3.0 * (TOK_DEV * 8) ** -0.5), 1.5, ((0, 128),), jnp.float32)
    saved_values = centred(arg_keys[6], (TOKEN_COUNT,), 1.0, 6.0, ((0, 128),), jnp.float32)
    episode_ends = draw_episode_ends(jax.random.fold_in(arg_keys[9], 71), 0)
    segment_ids = draw_segment_ids(jax.random.fold_in(arg_keys[9], 71), 0)
    return dict(queries=queries, key_head_rows=key_head_rows, value_head_rows=value_head_rows, out_cotangent=out_cotangent, value_readout=value_readout, rewards=rewards, saved_values=saved_values, episode_ends=episode_ends, segment_ids=segment_ids)


def head_probs(query_rows, key_rows, allowed):
    score_scale = 1.0 / math.sqrt(query_rows.shape[1])
    scores = jnp.dot(query_rows, key_rows.T, preferred_element_type=jnp.float32) * score_scale
    scores = jnp.where(allowed, scores, -jnp.inf)
    row_max = lax.optimization_barrier(jnp.max(scores, axis=1, keepdims=True))
    row_sum = lax.optimization_barrier(jnp.sum(jnp.exp(scores - row_max), axis=1, keepdims=True))
    log_total = row_max + jnp.log(row_sum)
    return jnp.exp(scores - log_total)

def head_forward(query_head, key_head, value_head, allowed):
    window_row_block = query_head.shape[0]
    half_rows = window_row_block // 2
    pieces = []
    for block_index in range(2):
        row_start = block_index * half_rows
        row_end = row_start + half_rows
        weights = head_probs(query_head[row_start:row_end], key_head[:row_end], allowed[row_start:row_end, :row_end])
        pieces.append(jnp.dot(weights.astype(jnp.bfloat16), value_head[:row_end], preferred_element_type=jnp.float32))
    return jnp.concatenate(pieces, axis=0)

def head_backward(query_head, key_head, value_head, grad_out, output_head, allowed):
    window_row_block = query_head.shape[0]
    half_rows = window_row_block // 2
    score_scale = 1.0 / math.sqrt(query_head.shape[1])
    query_parts = []
    key_total = jnp.zeros(key_head.shape, jnp.float32)
    value_total = jnp.zeros(value_head.shape, jnp.float32)
    for block_index in range(2):
        row_start = block_index * half_rows
        row_end = row_start + half_rows
        weights = head_probs(query_head[row_start:row_end], key_head[:row_end], allowed[row_start:row_end, :row_end])
        weights_low = weights.astype(jnp.bfloat16)
        grad_rows = grad_out[row_start:row_end]
        grad_probs = jnp.dot(grad_rows, value_head[:row_end].T, preferred_element_type=jnp.float32)
        row_dot = lax.optimization_barrier(jnp.sum(grad_rows.astype(jnp.float32) * output_head[row_start:row_end], axis=1, keepdims=True))
        grad_scores = (weights * (grad_probs - row_dot)).astype(jnp.bfloat16)
        query_parts.append(jnp.dot(grad_scores, key_head[:row_end], preferred_element_type=jnp.float32) * score_scale)
        key_part = lax.dot_general(grad_scores, query_head[row_start:row_end], (((0,), (0,)), ((), ())), preferred_element_type=jnp.float32) * score_scale
        value_part = lax.dot_general(weights_low, grad_rows, (((0,), (0,)), ((), ())), preferred_element_type=jnp.float32)
        key_total = key_total + jnp.pad(key_part, ((0, window_row_block - row_end), (0, 0)))
        value_total = value_total + jnp.pad(value_part, ((0, window_row_block - row_end), (0, 0)))
    return (jnp.concatenate(query_parts, axis=0), key_total, value_total)

def chain_returns(rewards, episode_ends):
    length = rewards.shape[0]
    position = jnp.arange(length)
    boundary = (position == length // 2 - 1) | (position == length - 1)
    keeping = jnp.where(boundary, 0, 1 - episode_ends).astype(jnp.float32)

    def backward_step(later, inputs):
        reward_now, keep_now = inputs
        current = reward_now + keep_now * later
        return (current, current)
    _, gains = lax.scan(backward_step, jnp.zeros((), jnp.float32), (rewards, keeping), reverse=True)
    return gains

def window_grads(queries, key_head_rows, value_head_rows, out_cotangent, value_readout, segment_ids, gains):
    window_row_block = queries.shape[0]
    group_width = QUERY_HEADS // KEY_VALUE_HEADS
    query_split = queries.reshape(window_row_block, QUERY_HEADS, HEAD_WIDTH).transpose(1, 0, 2)
    key_divided = key_head_rows.reshape(window_row_block, KEY_VALUE_HEADS, HEAD_WIDTH).transpose(1, 0, 2)
    value_divided = value_head_rows.reshape(window_row_block, KEY_VALUE_HEADS, HEAD_WIDTH).transpose(1, 0, 2)
    cotan_split = out_cotangent.reshape(window_row_block, QUERY_HEADS, HEAD_WIDTH).transpose(1, 0, 2)
    readout_split = value_readout.astype(jnp.float32).reshape(QUERY_HEADS, HEAD_WIDTH)
    position = jnp.arange(window_row_block)
    allowed = (position[None, :] <= position[:, None]) & (segment_ids[None, :] == segment_ids[:, None])

    def forward_head(h):
        return head_forward(query_split[h], key_divided[h // group_width], value_divided[h // group_width], allowed)
    outputs = lax.map(forward_head, jnp.arange(QUERY_HEADS))
    estimate = jnp.einsum('hwd,hd->w', outputs, readout_split, precision=lax.Precision.HIGHEST)
    value_error = estimate - gains

    def backward_head(h):
        grad_out = (cotan_split[h].astype(jnp.float32) + value_error[:, None] * readout_split[h][None, :]).astype(jnp.bfloat16)
        return head_backward(query_split[h], key_divided[h // group_width], value_divided[h // group_width], grad_out, outputs[h], allowed)
    query_parts, key_portions, value_portions = lax.map(backward_head, jnp.arange(QUERY_HEADS))
    query_grad = query_parts.astype(jnp.bfloat16).transpose(1, 0, 2).reshape(window_row_block, QUERY_HEADS * HEAD_WIDTH)
    key_gradient = key_portions.reshape(KEY_VALUE_HEADS, group_width, window_row_block, HEAD_WIDTH).sum(axis=1).astype(jnp.bfloat16)
    value_gradient = value_portions.reshape(KEY_VALUE_HEADS, group_width, window_row_block, HEAD_WIDTH).sum(axis=1).astype(jnp.bfloat16)
    key_gradient = key_gradient.transpose(1, 0, 2).reshape(window_row_block, KEY_VALUE_HEADS * HEAD_WIDTH)
    value_gradient = value_gradient.transpose(1, 0, 2).reshape(window_row_block, KEY_VALUE_HEADS * HEAD_WIDTH)
    return (query_grad, key_gradient, value_gradient)

def reference(queries, key_head_rows, value_head_rows, out_cotangent, value_readout, rewards, saved_values, episode_ends, segment_ids):
    gains = chain_returns(rewards, episode_ends)
    window_total_count = queries.shape[0] // WINDOW_LENGTH

    def per_window(w):
        row_start = w * WINDOW_LENGTH

        def window_of(source):
            return lax.dynamic_slice_in_dim(source, row_start, WINDOW_LENGTH, 0)
        return window_grads(window_of(queries), window_of(key_head_rows), window_of(value_head_rows), window_of(out_cotangent), value_readout, window_of(segment_ids), window_of(gains))
    query_grad, key_gradient, value_gradient = lax.map(per_window, jnp.arange(window_total_count, dtype=jnp.int32))
    query_grad = query_grad.reshape(window_total_count * WINDOW_LENGTH, QUERY_HEADS * HEAD_WIDTH)
    key_gradient = key_gradient.reshape(window_total_count * WINDOW_LENGTH, KEY_VALUE_HEADS * HEAD_WIDTH)
    value_gradient = value_gradient.reshape(window_total_count * WINDOW_LENGTH, KEY_VALUE_HEADS * HEAD_WIDTH)
    return (query_grad, key_gradient, value_gradient, gains - saved_values)
```

```python
import math

import jax
import jax.numpy as jnp
from jax import lax
from jax.experimental import pallas as pl
from jax.experimental.pallas import tpu as pltpu
from jax.sharding import PartitionSpec as P

MESH = pl.DeviceIdType.MESH
F32, BF16 = jnp.float32, jnp.bfloat16
D = 128
PEERS = 8
GROUP = 8
ROWS = PEERS * D
KEYS = 2 * ROWS
T = 256
NB = ROWS // T
SPLIT = 4
HEADS = GROUP // SPLIT
WIDE = HEADS * D
BIG = 1e30
SCALE = 1.0 / math.sqrt(D)
EXP2 = SCALE * math.log2(math.e)


def mm(a, b, dims=((1,), (0,))):
    return lax.dot_general(a, b, (dims, ((), ())), preferred_element_type=F32)


def ds(start, size):
    if isinstance(start, int):
        return pl.ds(start, size)
    return pl.ds(pl.multiple_of(start, size), size)


def kernel(
    q_in, k_in, v_in, g_in, readout_in, rewards_in, saved_in, ends_in, segs_in,
    dq_out, dk_out, dv_out, adv_out,
    q, g, dq, kaug, v, kt, vt, qm, probs, ohi, olo, dsc, sc, dka, dva, dkb, dvb, rk, rv,
    pk, tot, est, es, inv, rcol, vet, rd,
    q_s, q_r, g_s, g_r, d_s, d_r, kv_s, kv_r, x_s, x_r, pk_s, pk_r, tot_s, tot_r, es_s, es_r, o_s, o_r, loc,
):
    me = lax.axis_index("dp")
    sq = lax.axis_index("seq")
    seqs = lax.axis_size("seq")
    x = lax.div(me, PEERS)
    hd = lax.rem(me, PEERS)
    late = x == 1

    def dev(half, place):
        return (half * PEERS + place, sq)

    def nxt(k):
        return lax.rem(hd + k, PEERS)

    def send(src, dst, ssem, rsem, device):
        return pltpu.make_async_remote_copy(
            src_ref=src, dst_ref=dst, send_sem=ssem, recv_sem=rsem, device_id=device, device_id_type=MESH
        )

    barrier = pltpu.get_barrier_semaphore()
    for k in range(1, 16):
        pl.semaphore_signal(barrier, inc=1, device_id=(lax.rem(me + k, 16), sq), device_id_type=MESH)
    for k in (1, seqs - 1):
        pl.semaphore_signal(barrier, inc=1, device_id=(me, lax.rem(sq + k, seqs)), device_id_type=MESH)
    pl.semaphore_wait(barrier, 17)

    def kv_copy(k, t):
        src, dst = ((k_in, kaug), (v_in, v))[t]
        p = nxt(k)
        return send(
            src.at[:, ds(p * D, D)], dst.at[ds(ROWS + hd * D, D), pl.ds(0, D)], kv_s.at[t, k], kv_r.at[t, k], dev(x, p)
        )

    def kv_local(t):
        src, dst = ((k_in, kaug), (v_in, v))[t]
        return pltpu.make_async_copy(src.at[:, ds(hd * D, D)], dst.at[ds(ROWS + hd * D, D), pl.ds(0, D)], kv_r.at[t, 0])

    def in_copy(src, dst, ssem, rsem, part, k):
        p = nxt(k)
        return send(
            src.at[:, ds((p * SPLIT + part) * WIDE, WIDE)],
            dst.at[ds(hd * D, D), ds(part * WIDE, WIDE)],
            ssem.at[part, k], rsem.at[part, k], dev(x, p),
        )

    def in_local(src, dst, rsem, part):
        return pltpu.make_async_copy(
            src.at[:, ds((hd * SPLIT + part) * WIDE, WIDE)], dst.at[ds(hd * D, D), ds(part * WIDE, WIDE)], rsem.at[part, 0]
        )

    def start_in(src, dst, ssem, rsem, part):
        in_local(src, dst, rsem, part).start()
        for k in range(1, PEERS):
            in_copy(src, dst, ssem, rsem, part, k).start()

    def wait_in(src, dst, ssem, rsem, part):
        in_local(src, dst, rsem, part).wait()
        for k in range(1, PEERS):
            in_copy(src, dst, ssem, rsem, part, k).wait_recv()

    for t in range(2):
        kv_local(t).start()
        for k in range(1, PEERS):
            kv_copy(k, t).start()

    sub = lax.broadcasted_iota(jnp.int32, (D, D), 0)
    lane = lax.broadcasted_iota(jnp.int32, (D, D), 1)
    lane_f = lane.astype(F32)

    def wide(row):
        return jnp.broadcast_to(row, (D, D))

    def column(row):
        return wide(row).T

    last = jnp.logical_and(me == 15, jnp.logical_or(sq == seqs // 2 - 1, sq == seqs - 1))
    ends = ends_in[...].astype(F32)
    row_lane = lax.broadcasted_iota(jnp.int32, (1, D), 1)
    ends = jnp.where(jnp.logical_and(row_lane == D - 1, last), 1.0, ends)
    ends_col = column(ends)
    before = jnp.sum(jnp.where(sub < lane, ends_col, 0.0), axis=0, keepdims=True)
    total_ends = jnp.sum(ends, axis=1, keepdims=True)
    reach = jnp.logical_and(sub >= lane, column(before) == wide(before))
    local_gain = jnp.sum(jnp.where(reach, column(rewards_in[...]), 0.0), axis=0, keepdims=True)
    passing = (total_ends - before == 0).astype(F32)
    through = (total_ends == 0).astype(F32)
    pk[me, 0:1, :] = segs_in[...].astype(F32)
    pk[me, 1:2, :] = jnp.broadcast_to(through, (1, D))
    pk[me, 2:3, :] = jnp.broadcast_to(local_gain[:, 0:1], (1, D))

    def pk_copy(k):
        return send(pk.at[me], pk.at[me], pk_s.at[k], pk_r.at[k], (lax.rem(me + k, 16), sq))

    for k in range(1, 16):
        pk_copy(k).start()

    start_in(q_in, q, q_s, q_r, 0)
    start_in(q_in, q, q_s, q_r, 1)

    for h in range(GROUP):
        rcol[h] = column(readout_in[h : h + 1, :])
    est[...] = jnp.zeros_like(est)
    dka[...] = jnp.zeros_like(dka)
    dva[...] = jnp.zeros_like(dva)

    for k in range(1, 16):
        pk_copy(k).wait()

    def fold(value, lowest):
        for d in range(15, -1, -1):
            joined = pk[d, 2:3, :] + pk[d, 1:2, :] * value
            value = joined if lowest is None else jnp.where(d >= lowest, joined, value)
        return value

    tot[0] = jnp.broadcast_to(fold(jnp.zeros((1, D), F32), None), (8, D))
    tot_copy = send(tot.at[0], tot.at[1], tot_s, tot_r, (me, lax.rem(sq + seqs - 1, seqs)))
    tot_copy.start()

    for t in range(2):
        kv_local(t).wait()
        for k in range(1, PEERS):
            kv_copy(k, t).wait_recv()

    def x_copy(t):
        dst = (kaug, v)[t]
        return send(
            dst.at[pl.ds(ROWS, ROWS), pl.ds(0, D)], dst.at[pl.ds(0, ROWS), pl.ds(0, D)], x_s.at[t], x_r.at[t], dev(1 - x, hd)
        )

    @pl.when(x == 0)
    def _():
        for t in range(2):
            x_copy(t).start()
        kaug[0:ROWS, 0:D] = jnp.zeros((ROWS, D), BF16)
        v[0:ROWS, :] = jnp.zeros((ROWS, D), BF16)

    start_in(q_in, q, q_s, q_r, 2)
    start_in(q_in, q, q_s, q_r, 3)

    first = pk[0, 0:1, 0:1]

    def seg_block(b, carry):
        own = b >= PEERS
        place = jnp.where(own, x * PEERS + b - PEERS, (1 - x) * PEERS + b)
        code = column(pk[place, 0:1, :] - first)
        hidden = jnp.logical_and(jnp.logical_not(own), x == 0)
        code = jnp.where(hidden, 100.0, code)
        kaug[ds(b * D, D), D : 2 * D] = jnp.where(code == lane_f, 1.0, 0.0).astype(BF16)
        return carry

    lax.fori_loop(0, 2 * PEERS, seg_block, 0)

    def row_block(b, carry):
        code = column(pk[x * PEERS + b, 0:1, :] - first)
        qm[ds(b * D, D), :] = jnp.where(code == lane_f, 0.0, -BIG).astype(BF16)
        return carry

    lax.fori_loop(0, PEERS, row_block, 0)

    @pl.when(late)
    def _():
        for t in range(2):
            x_copy(t).wait_recv()

    for b in range(2 * PEERS):
        kt[:, b * D : (b + 1) * D] = kaug[b * D : (b + 1) * D, 0:D].T
        vt[:, b * D : (b + 1) * D] = v[b * D : (b + 1) * D, :].T

    tile_sub = lax.broadcasted_iota(jnp.int32, (T, T), 0)
    tile_lane = lax.broadcasted_iota(jnp.int32, (T, T), 1)

    def forward(h):
        cols = ds(h * D, D)
        for i in range(NB):
            r = slice(i * T, (i + 1) * T)
            count = NB + i + 1
            qa = jnp.concatenate([q[r, cols], qm[r, :]], axis=1)
            top = None
            for j in range(count):
                s = mm(kaug[j * T : (j + 1) * T, :], qa, ((1,), (1,)))
                if j == count - 1:
                    s = jnp.where(tile_sub <= tile_lane, s, -BIG)
                sc[i % 2, j * T : (j + 1) * T, :] = s
                part = jnp.max(s.reshape(T // 8, 8, T), axis=0)
                top = part if top is None else jnp.maximum(top, part)
            top = jnp.max(top, axis=0, keepdims=True) * EXP2
            total = None
            for j in range(count):
                p = jnp.exp2(sc[i % 2, j * T : (j + 1) * T, :] * EXP2 - top)
                part = jnp.sum(p.reshape(T // 8, 8, T), axis=0)
                total = part if total is None else total + part
                probs[h, j * T : (j + 1) * T, r] = p.astype(BF16)
            scale = 1.0 / jnp.sum(total, axis=0, keepdims=True)
            n = count * T
            out = mm(vt[:, 0:n], probs[h, 0:n, r]) * scale
            high = out.astype(BF16)
            ohi[h, :, r] = high
            olo[h, :, r] = (out - high.astype(F32)).astype(BF16)
            for c in range(T // D):
                b = i * (T // D) + c
                half = slice(c * D, (c + 1) * D)
                est[b : b + 1, :] += jnp.sum(out[:, half] * rcol[h], axis=0, keepdims=True)
                inv[h, b : b + 1, :] = scale[:, half]

    def forward_part(part, carry):
        wait_in(q_in, q, q_s, q_r, part)

        @pl.when(part >= 1)
        def _():
            start_in(g_in, g, g_s, g_r, part - 1)

        lax.fori_loop(0, HEADS, lambda n, c: (forward(part * HEADS + n), c)[1], 0)
        return carry

    lax.fori_loop(0, SPLIT, forward_part, 0)

    tot_copy.wait()
    beyond = tot[1, 0:1, :]
    gains = local_gain + passing * fold(beyond, me + 1)
    adv_out[...] = gains - saved_in[...]
    place_sub = lax.broadcasted_iota(jnp.int32, (PEERS, D), 0)
    es[hd] = est[...] - jnp.where(place_sub == hd, jnp.broadcast_to(gains, (PEERS, D)), 0.0)

    def es_copy(k):
        return send(es.at[hd], es.at[hd], es_s.at[k], es_r.at[k], dev(x, nxt(k)))

    for k in range(1, PEERS):
        es_copy(k).start()
    start_in(g_in, g, g_s, g_r, SPLIT - 1)
    for k in range(1, PEERS):
        es_copy(k).wait()
    error = es[0]
    for d in range(1, PEERS):
        error = error + es[d]
    vet[...] = jnp.concatenate([error] * (D // PEERS), axis=0).T

    def backward(h):
        cols = ds(h * D, D)
        scales = jnp.concatenate([inv[h]] * (D // PEERS), axis=0).T
        readout = readout_in[pl.ds(h, 1), :]
        for b in range(PEERS):
            r = slice(b * D, (b + 1) * D)
            grad = g[r, cols].astype(F32) + vet[:, b : b + 1] * readout
            grad = (grad * scales[:, b : b + 1]).astype(BF16)
            g[r, cols] = grad
            cross = mm(grad, ohi[h, :, r]) + mm(grad, olo[h, :, r])
            rd[:, r] = jnp.broadcast_to(jnp.sum(jnp.where(sub == lane, cross, 0.0), axis=0, keepdims=True), (8, D))
        for i in range(NB):
            r = slice(i * T, (i + 1) * T)
            count = NB + i + 1
            grad = g[r, cols]
            dot = rd[0:1, r]
            for j in range(count):
                a = slice(j * T, (j + 1) * T)
                dp = mm(v[a, :], grad, ((1,), (1,)))
                dsc[a, r] = (probs[h, a, r].astype(F32) * (dp - dot)).astype(BF16)
            n = count * T
            out = mm(kt[:, 0:n], dsc[0:n, r]) * SCALE
            dq[r, cols] = out.T.astype(BF16)
        for j in range(2 * NB):
            a = slice(j * T, (j + 1) * T)
            low = max(0, j - NB) * T
            dva[a, :] += mm(probs[h, a, low:ROWS], g[low:ROWS, cols])
            dka[a, :] += mm(dsc[a, low:ROWS], q[low:ROWS, cols])

    def dq_copy(part, k):
        p = nxt(k)
        return send(
            dq.at[ds(p * D, D), ds(part * WIDE, WIDE)],
            dq_out.at[:, ds((hd * SPLIT + part) * WIDE, WIDE)],
            d_s.at[part, k], d_r.at[part, k], dev(x, p),
        )

    def dq_local(part):
        return pltpu.make_async_copy(
            dq.at[ds(hd * D, D), ds(part * WIDE, WIDE)], dq_out.at[:, ds((hd * SPLIT + part) * WIDE, WIDE)], d_r.at[part, 0]
        )

    def backward_part(part, carry):
        wait_in(g_in, g, g_s, g_r, part)
        lax.fori_loop(0, HEADS, lambda n, c: (backward(part * HEADS + n), c)[1], 0)
        dq_local(part).start()
        for k in range(1, PEERS):
            dq_copy(part, k).start()
        return carry

    lax.fori_loop(0, SPLIT, backward_part, 0)

    dkb[...] = (dka[...] * SCALE).astype(BF16)
    dvb[...] = dva[...].astype(BF16)

    def out_copy(t, k, same):
        src, dst = ((dkb, rk), (dvb, rv))[t]
        p = nxt(k)
        base = ROWS if same else 0
        slot = 1 if same else 0
        index = k + (0 if same else PEERS)
        return send(
            src.at[ds(base + p * D, D), :], dst.at[slot, :, ds(hd * D, D)], o_s.at[t, index], o_r.at[t, index],
            dev(x if same else 1 - x, p),
        )

    @pl.when(late)
    def _():
        for k in range(PEERS):
            for t in range(2):
                out_copy(t, k, False).start()

    def out_local(t):
        src, dst = ((dkb, rk), (dvb, rv))[t]
        return pltpu.make_async_copy(src.at[ds(ROWS + hd * D, D), :], dst.at[1, :, ds(hd * D, D)], loc.at[t])

    for t in range(2):
        out_local(t).start()
        for k in range(1, PEERS):
            out_copy(t, k, True).start()
    for t in range(2):
        out_local(t).wait()
        for k in range(1, PEERS):
            out_copy(t, k, True).wait()

    @pl.when(late)
    def _():
        for t in range(2):
            for k in range(PEERS):
                out_copy(t, k, False).wait_send()
        dk_out[...] = rk[1]
        dv_out[...] = rv[1]

    @pl.when(x == 0)
    def _():
        for t in range(2):
            for k in range(PEERS):
                out_copy(t, k, False).wait_recv()
            x_copy(t).wait_send()
        dk_out[...] = (rk[0].astype(F32) + rk[1].astype(F32)).astype(BF16)
        dv_out[...] = (rv[0].astype(F32) + rv[1].astype(F32)).astype(BF16)

    for t in range(2):
        for k in range(1, PEERS):
            kv_copy(k, t).wait_send()
    for part in range(SPLIT):
        dq_local(part).wait()
        for k in range(1, PEERS):
            in_copy(q_in, q, q_s, q_r, part, k).wait_send()
            in_copy(g_in, g, g_s, g_r, part, k).wait_send()
            dq_copy(part, k).wait()


def body(queries, keys, values, cotangent, readout, rewards, saved, ends, segs):
    place = lax.rem(lax.axis_index("dp"), PEERS)
    heads = lax.dynamic_slice_in_dim(readout.reshape(PEERS * GROUP, D), place * GROUP, GROUP, 0).astype(F32)
    vmem = pl.BlockSpec(memory_space=pltpu.VMEM)
    hbm = pl.BlockSpec(memory_space=pl.ANY)
    dma = pltpu.SemaphoreType.DMA
    grads = pl.pallas_call(
        kernel,
        out_shape=(
            jax.ShapeDtypeStruct(queries.shape, BF16),
            jax.ShapeDtypeStruct(keys.shape, BF16),
            jax.ShapeDtypeStruct(values.shape, BF16),
            jax.ShapeDtypeStruct((1, D), F32),
        ),
        in_specs=[hbm, hbm, hbm, hbm, vmem, vmem, vmem, vmem, vmem],
        out_specs=(hbm, vmem, vmem, vmem),
        scratch_shapes=[
            pltpu.VMEM((ROWS, ROWS), BF16),
            pltpu.VMEM((ROWS, ROWS), BF16),
            pltpu.VMEM((ROWS, ROWS), BF16),
            pltpu.VMEM((KEYS, 2 * D), BF16),
            pltpu.VMEM((KEYS, D), BF16),
            pltpu.VMEM((D, KEYS), BF16),
            pltpu.VMEM((D, KEYS), BF16),
            pltpu.VMEM((ROWS, D), BF16),
            pltpu.VMEM((GROUP, KEYS, ROWS), BF16),
            pltpu.VMEM((GROUP, D, ROWS), BF16),
            pltpu.VMEM((GROUP, D, ROWS), BF16),
            pltpu.VMEM((KEYS, ROWS), BF16),
            pltpu.VMEM((2, KEYS, T), F32),
            pltpu.VMEM((KEYS, D), F32),
            pltpu.VMEM((KEYS, D), F32),
            pltpu.VMEM((KEYS, D), BF16),
            pltpu.VMEM((KEYS, D), BF16),
            pltpu.VMEM((2, D, ROWS), BF16),
            pltpu.VMEM((2, D, ROWS), BF16),
            pltpu.VMEM((16, 8, D), F32),
            pltpu.VMEM((2, 8, D), F32),
            pltpu.VMEM((PEERS, D), F32),
            pltpu.VMEM((PEERS, PEERS, D), F32),
            pltpu.VMEM((GROUP, PEERS, D), F32),
            pltpu.VMEM((GROUP, D, D), F32),
            pltpu.VMEM((D, D), F32),
            pltpu.VMEM((8, ROWS), F32),
            dma((SPLIT, PEERS)), dma((SPLIT, PEERS)),
            dma((SPLIT, PEERS)), dma((SPLIT, PEERS)),
            dma((SPLIT, PEERS)), dma((SPLIT, PEERS)),
            dma((2, PEERS)), dma((2, PEERS)),
            dma((2,)), dma((2,)),
            dma((16,)), dma((16,)),
            dma, dma,
            dma((PEERS,)), dma((PEERS,)),
            dma((2, 2 * PEERS)), dma((2, 2 * PEERS)),
            dma((2,)),
        ],
        compiler_params=pltpu.CompilerParams(
            collective_id=0, has_side_effects=True, vmem_limit_bytes=62 << 20
        ),
    )(
        queries, keys, values, cotangent, heads,
        rewards.reshape(1, D), saved.reshape(1, D), ends.reshape(1, D), segs.reshape(1, D),
    )
    return (grads[0], grads[1], grads[2], grads[3].reshape(D))


def solution(mesh):
    rows, flat = P(("seq", "dp"), None), P(("seq", "dp"))
    return jax.shard_map(
        body,
        mesh=mesh,
        in_specs=(rows, rows, rows, rows, P(), flat, flat, flat, flat),
        out_specs=(rows, rows, rows, flat),
        check_vma=False,
    )
```

```python
import math

import jax
import jax.numpy as jnp
from jax import lax
from jax.experimental import pallas as pl
from jax.experimental.pallas import tpu as pltpu
from jax.sharding import PartitionSpec as P

MESH = pl.DeviceIdType.MESH
F32, BF16 = jnp.float32, jnp.bfloat16
D = 128
PEERS = 8
GROUP = 8
ROWS = PEERS * D
KEYS = 2 * ROWS
T = 256
NB = ROWS // T
SPLIT = 4
HEADS = GROUP // SPLIT
WIDE = HEADS * D
BIG = 1e30
SCALE = 1.0 / math.sqrt(D)
EXP2 = SCALE * math.log2(math.e)


def mm(a, b, dims=((1,), (0,))):
    return lax.dot_general(a, b, (dims, ((), ())), preferred_element_type=F32)


def ds(start, size):
    if isinstance(start, int):
        return pl.ds(start, size)
    return pl.ds(pl.multiple_of(start, size), size)


def kernel(
    q_in, k_in, v_in, g_in, readout_in, rewards_in, saved_in, ends_in, segs_in,
    dq_out, dk_out, dv_out, adv_out,
    q, g, dq, kaug, v, kt, vt, qm, probs, ohi, olo, dsc, sc, dka, dva, dkb, dvb, rk, rv,
    pk, tot, est, es, inv, rcol, vet, rd,
    q_s, q_r, g_s, g_r, d_s, d_r, kv_s, kv_r, x_s, x_r, pk_s, pk_r, tot_s, tot_r, es_s, es_r, o_s, o_r, loc,
):
    me = lax.axis_index("dp")
    sq = lax.axis_index("seq")
    seqs = lax.axis_size("seq")
    x = lax.div(me, PEERS)
    hd = lax.rem(me, PEERS)
    late = x == 1

    def dev(half, place):
        return (half * PEERS + place, sq)

    def nxt(k):
        return lax.rem(hd + k, PEERS)

    def send(src, dst, ssem, rsem, device):
        return pltpu.make_async_remote_copy(
            src_ref=src, dst_ref=dst, send_sem=ssem, recv_sem=rsem, device_id=device, device_id_type=MESH
        )

    def readout_row(h):
        return readout_in[:, ds((hd * GROUP + h) * D, D)].astype(F32)

    barrier = pltpu.get_barrier_semaphore()
    for k in range(1, 16):
        pl.semaphore_signal(barrier, inc=1, device_id=(lax.rem(me + k, 16), sq), device_id_type=MESH)
    for k in (1, seqs - 1):
        pl.semaphore_signal(barrier, inc=1, device_id=(me, lax.rem(sq + k, seqs)), device_id_type=MESH)

    def kv_copy(k, t):
        src, dst = ((k_in, kaug), (v_in, v))[t]
        p = nxt(k)
        return send(
            src.at[:, ds(p * D, D)], dst.at[ds(ROWS + hd * D, D), pl.ds(0, D)], kv_s.at[t, k], kv_r.at[t, k], dev(x, p)
        )

    def kv_local(t):
        src, dst = ((k_in, kaug), (v_in, v))[t]
        return pltpu.make_async_copy(src.at[:, ds(hd * D, D)], dst.at[ds(ROWS + hd * D, D), pl.ds(0, D)], kv_r.at[t, 0])

    def in_copy(src, dst, ssem, rsem, part, k):
        p = nxt(k)
        return send(
            src.at[:, ds((p * SPLIT + part) * WIDE, WIDE)],
            dst.at[ds(hd * D, D), ds(part * WIDE, WIDE)],
            ssem.at[part, k], rsem.at[part, k], dev(x, p),
        )

    def in_local(src, dst, rsem, part):
        return pltpu.make_async_copy(
            src.at[:, ds((hd * SPLIT + part) * WIDE, WIDE)], dst.at[ds(hd * D, D), ds(part * WIDE, WIDE)], rsem.at[part, 0]
        )

    def start_in(src, dst, ssem, rsem, part):
        in_local(src, dst, rsem, part).start()
        for k in range(1, PEERS):
            in_copy(src, dst, ssem, rsem, part, k).start()

    def wait_in(src, dst, ssem, rsem, part):
        in_local(src, dst, rsem, part).wait()
        for k in range(1, PEERS):
            in_copy(src, dst, ssem, rsem, part, k).wait_recv()

    def x_copy(t, k):
        src, dst = ((k_in, kaug), (v_in, v))[t]
        p = nxt(k)
        return send(
            src.at[:, ds(p * D, D)], dst.at[ds(hd * D, D), pl.ds(0, D)], x_s.at[t, k], x_r.at[t, k], dev(1 - x, p)
        )

    sub = lax.broadcasted_iota(jnp.int32, (D, D), 0)
    lane = lax.broadcasted_iota(jnp.int32, (D, D), 1)
    lane_f = lane.astype(F32)

    def wide(row):
        return jnp.broadcast_to(row, (D, D))

    def column(row):
        return wide(row).T

    last = jnp.logical_and(me == 15, jnp.logical_or(sq == seqs // 2 - 1, sq == seqs - 1))
    ends = ends_in[...].astype(F32)
    row_lane = lax.broadcasted_iota(jnp.int32, (1, D), 1)
    ends = jnp.where(jnp.logical_and(row_lane == D - 1, last), 1.0, ends)
    ends_col = column(ends)
    before = jnp.sum(jnp.where(sub < lane, ends_col, 0.0), axis=0, keepdims=True)
    total_ends = jnp.sum(ends, axis=1, keepdims=True)
    reach = jnp.logical_and(sub >= lane, column(before) == wide(before))
    local_gain = jnp.sum(jnp.where(reach, column(rewards_in[...]), 0.0), axis=0, keepdims=True)
    passing = (total_ends - before == 0).astype(F32)
    through = (total_ends == 0).astype(F32)
    pk[me, 0:1, :] = segs_in[...].astype(F32)
    pk[me, 1:2, :] = jnp.broadcast_to(through, (1, D))
    pk[me, 2:3, :] = jnp.broadcast_to(local_gain[:, 0:1], (1, D))

    def pk_copy(k):
        return send(pk.at[me], pk.at[me], pk_s.at[k], pk_r.at[k], (lax.rem(me + k, 16), sq))

    pl.semaphore_wait(barrier, 17)
    for k in range(1, 16):
        pk_copy(k).start()
    for t in range(2):
        kv_local(t).start()
        for k in range(1, PEERS):
            kv_copy(k, t).start()

    @pl.when(x == 0)
    def _():
        for t in range(2):
            for k in range(PEERS):
                x_copy(t, k).start()

    for part in range(SPLIT):
        start_in(q_in, q, q_s, q_r, part)

    @pl.when(x == 0)
    def _():
        kaug[0:ROWS, 0:D] = jnp.zeros((ROWS, D), BF16)
        v[0:ROWS, :] = jnp.zeros((ROWS, D), BF16)

    for h in range(GROUP):
        rcol[h] = column(readout_row(h))
    est[...] = jnp.zeros_like(est)
    dka[...] = jnp.zeros_like(dka)
    dva[...] = jnp.zeros_like(dva)

    for k in range(1, 16):
        pk_copy(k).wait()

    def fold(value, lowest):
        for d in range(15, -1, -1):
            joined = pk[d, 2:3, :] + pk[d, 1:2, :] * value
            value = joined if lowest is None else jnp.where(d >= lowest, joined, value)
        return value

    tot[0] = jnp.broadcast_to(fold(jnp.zeros((1, D), F32), None), (8, D))
    tot_copy = send(tot.at[0], tot.at[1], tot_s, tot_r, (me, lax.rem(sq + seqs - 1, seqs)))
    tot_copy.start()

    lines = [pk[(1 - x) * PEERS + b, 0:1, :] for b in range(PEERS)] + [pk[x * PEERS + b, 0:1, :] for b in range(PEERS)]
    codes = (jnp.concatenate(lines * (D // 16), axis=0) - pk[0, 0:1, 0:1]).T
    for b in range(2 * PEERS):
        code = jnp.broadcast_to(codes[:, b : b + 1], (D, D))
        if b < PEERS:
            code = jnp.where(x == 0, 100.0, code)
        else:
            qm[(b - PEERS) * D : (b - PEERS + 1) * D, :] = jnp.where(code == lane_f, 0.0, -BIG).astype(BF16)
        kaug[b * D : (b + 1) * D, D : 2 * D] = jnp.where(code == lane_f, 1.0, 0.0).astype(BF16)

    for t in range(2):
        kv_local(t).wait()
        for k in range(1, PEERS):
            kv_copy(k, t).wait_recv()

    @pl.when(late)
    def _():
        for t in range(2):
            for k in range(PEERS):
                x_copy(t, k).wait_recv()

    for b in range(2 * PEERS):
        vt[:, b * D : (b + 1) * D] = v[b * D : (b + 1) * D, :].T

    tile_sub = lax.broadcasted_iota(jnp.int32, (T, T), 0)
    tile_lane = lax.broadcasted_iota(jnp.int32, (T, T), 1)

    def forward(heads):
        steps = [(h, i) for h in heads for i in range(NB)]
        state = {}

        def score(t, j):
            h, i = steps[t]
            cols, r = ds(h * D, D), slice(i * T, (i + 1) * T)
            if j == 0:
                state["q", t] = jnp.concatenate([q[r, cols], qm[r, :]], axis=1)
            s = mm(kaug[j * T : (j + 1) * T, :], state["q", t], ((1,), (1,)))
            if j == NB + i:
                s = jnp.where(tile_sub <= tile_lane, s, -BIG)
            sc[t % 2, j * T : (j + 1) * T, :] = s
            part = jnp.max(s.reshape(T // 8, 8, T), axis=0)
            state["top", t] = part if j == 0 else jnp.maximum(state["top", t], part)
            if j == NB + i:
                state["top", t] = jnp.max(state["top", t], axis=0, keepdims=True) * EXP2

        def weigh(t, j):
            h, i = steps[t]
            r = slice(i * T, (i + 1) * T)
            p = jnp.exp2(sc[t % 2, j * T : (j + 1) * T, :] * EXP2 - state["top", t])
            part = jnp.sum(p.reshape(T // 8, 8, T), axis=0)
            state["sum", t] = part if j == 0 else state["sum", t] + part
            probs[h, j * T : (j + 1) * T, r] = p.astype(BF16)

        def output(t):
            h, i = steps[t]
            r, n = slice(i * T, (i + 1) * T), (NB + i + 1) * T
            scale = 1.0 / jnp.sum(state["sum", t], axis=0, keepdims=True)
            out = mm(vt[:, 0:n], probs[h, 0:n, r]) * scale
            high = out.astype(BF16)
            ohi[h, :, r] = high
            olo[h, :, r] = (out - high.astype(F32)).astype(BF16)
            for c in range(T // D):
                b = i * (T // D) + c
                half = slice(c * D, (c + 1) * D)
                est[b : b + 1, :] += jnp.sum(out[:, half] * rcol[h], axis=0, keepdims=True)
                inv[h, b : b + 1, :] = scale[:, half]

        for t in range(len(steps) + 2):
            if t >= 2:
                output(t - 2)
            for j in range(2 * NB):
                if t < len(steps) and j <= NB + steps[t][1]:
                    score(t, j)
                if 1 <= t <= len(steps) and j <= NB + steps[t - 1][1]:
                    weigh(t - 1, j)

    def forward_part(part, carry):
        wait_in(q_in, q, q_s, q_r, part)

        @pl.when(part >= 2)
        def _():
            start_in(g_in, g, g_s, g_r, part - 2)

        forward([part * HEADS + n for n in range(HEADS)])
        return carry

    lax.fori_loop(0, SPLIT, forward_part, 0)

    tot_copy.wait()
    beyond = tot[1, 0:1, :]
    gains = local_gain + passing * fold(beyond, me + 1)
    adv_out[...] = gains - saved_in[...]
    place_sub = lax.broadcasted_iota(jnp.int32, (PEERS, D), 0)
    es[hd] = est[...] - jnp.where(place_sub == hd, jnp.broadcast_to(gains, (PEERS, D)), 0.0)

    def es_copy(k):
        return send(es.at[hd], es.at[hd], es_s.at[k], es_r.at[k], dev(x, nxt(k)))

    for k in range(1, PEERS):
        es_copy(k).start()
    for part in range(SPLIT - 2, SPLIT):
        start_in(g_in, g, g_s, g_r, part)
    for b in range(2 * PEERS):
        kt[:, b * D : (b + 1) * D] = kaug[b * D : (b + 1) * D, 0:D].T
    for k in range(1, PEERS):
        es_copy(k).wait()
    error = es[0]
    for d in range(1, PEERS):
        error = error + es[d]
    vet[...] = jnp.concatenate([error] * (D // PEERS), axis=0).T

    def prepare(n, h):
        cols = ds(h * D, D)
        scales = jnp.concatenate([inv[h]] * (D // PEERS), axis=0).T
        readout = readout_row(h)

        def block(b):
            r = slice(b * D, (b + 1) * D)
            grad = g[r, cols].astype(F32) + vet[:, b : b + 1] * readout
            grad = (grad * scales[:, b : b + 1]).astype(BF16)
            g[r, cols] = grad
            cross = mm(grad, ohi[h, :, r]) + mm(grad, olo[h, :, r])
            rd[n, :, r] = jnp.broadcast_to(jnp.sum(jnp.where(sub == lane, cross, 0.0), axis=0, keepdims=True), (8, D))

        return [(block, (b,)) for b in range(PEERS)]

    def units(n, h, own):
        cols = ds(h * D, D)
        base = ROWS if own else 0

        def grads(i, j):
            r, a = slice(i * T, (i + 1) * T), slice(base + j * T, base + (j + 1) * T)
            c = slice(n * ROWS + j * T, n * ROWS + (j + 1) * T)
            dp = mm(v[a, :], g[r, cols], ((1,), (1,)))
            dsc[c, r] = (probs[h, a, r].astype(F32) * (dp - rd[n, 0:1, r])).astype(BF16)
            count = i + 1 if own else NB
            if j == count - 1:
                out = mm(kt[:, base : base + count * T], dsc[n * ROWS : n * ROWS + count * T, r])
                keep = slice(i * D, (i + 1) * D)
                if own:
                    dq[r, cols] = ((sc[n, keep, :] + out) * SCALE).T.astype(BF16)
                else:
                    sc[n, keep, :] = out

        def value(j):
            a, low = slice(base + j * T, base + (j + 1) * T), j * T if own else 0
            dva[a, :] += mm(probs[h, a, low:ROWS], g[low:ROWS, cols])

        def key(j):
            a, low = slice(base + j * T, base + (j + 1) * T), j * T if own else 0
            c = slice(n * ROWS + j * T, n * ROWS + (j + 1) * T)
            dka[a, :] += mm(dsc[c, low:ROWS], q[low:ROWS, cols])

        first = [(grads, (i, j)) for i in range(NB) for j in range(i + 1 if own else NB)]
        return first, [(value, (j,)) for j in range(NB)], [(key, (j,)) for j in range(NB)]

    def blend(long, short):
        taken = 0
        for index, (unit, arg) in enumerate(long):
            unit(*arg)
            while taken < len(short) and taken * len(long) < (index + 1) * len(short):
                short[taken][0](*short[taken][1])
                taken += 1

    def dq_copy(h, k):
        p = nxt(k)
        return send(
            dq.at[ds(p * D, D), ds(h * D, D)], dq_out.at[:, ds((hd * GROUP + h) * D, D)], d_s.at[h, k], d_r.at[h, k], dev(x, p)
        )

    def dq_local(h):
        return pltpu.make_async_copy(
            dq.at[ds(hd * D, D), ds(h * D, D)], dq_out.at[:, ds((hd * GROUP + h) * D, D)], d_r.at[h, 0]
        )

    def run(list_of_units):
        for unit, arg in list_of_units:
            unit(*arg)

    def backward_half(heads, own):
        if not own:
            run(prepare(0, heads[0]))
        pending = []
        for n, h in enumerate(heads):
            first, values, keys = units(n, h, own)
            ahead = prepare(n + 1, heads[n + 1]) if not own and n + 1 < len(heads) else []
            blend(first, ahead + values + pending)
            pending = keys
            if own:
                dq_local(h).start()
                for k in range(1, PEERS):
                    dq_copy(h, k).start()
        return pending

    def out_copy(t, k, same):
        src, dst = ((dkb, rk), (dvb, rv))[t]
        p, slot = nxt(k), 1 if same else 0
        return send(
            src.at[ds(slot * ROWS + p * D, D), :], dst.at[slot, :, ds(hd * D, D)],
            o_s.at[t, slot, k], o_r.at[t, slot, k], dev(x if same else 1 - x, p),
        )

    def backward_part(part, carry):
        wait_in(g_in, g, g_s, g_r, part)
        heads = [part * HEADS + n for n in range(HEADS)]
        run(backward_half(heads, False))

        @pl.when(jnp.logical_and(late, part == SPLIT - 1))
        def _():
            dkb[0:ROWS, :] = (dka[0:ROWS, :] * SCALE).astype(BF16)
            dvb[0:ROWS, :] = dva[0:ROWS, :].astype(BF16)
            for t in range(2):
                for k in range(PEERS):
                    out_copy(t, k, False).start()

        run(backward_half(heads, True))
        return carry

    lax.fori_loop(0, SPLIT, backward_part, 0)

    dkb[ROWS:KEYS, :] = (dka[ROWS:KEYS, :] * SCALE).astype(BF16)
    dvb[ROWS:KEYS, :] = dva[ROWS:KEYS, :].astype(BF16)

    def out_local(t):
        src, dst = ((dkb, rk), (dvb, rv))[t]
        return pltpu.make_async_copy(src.at[ds(ROWS + hd * D, D), :], dst.at[1, :, ds(hd * D, D)], loc.at[t])

    for t in range(2):
        out_local(t).start()
        for k in range(1, PEERS):
            out_copy(t, k, True).start()
    for t in range(2):
        out_local(t).wait()
        for k in range(1, PEERS):
            out_copy(t, k, True).wait()

    @pl.when(late)
    def _():
        for t in range(2):
            for k in range(PEERS):
                out_copy(t, k, False).wait_send()
        dk_out[...] = rk[1]
        dv_out[...] = rv[1]

    @pl.when(x == 0)
    def _():
        for t in range(2):
            for k in range(PEERS):
                out_copy(t, k, False).wait_recv()
                x_copy(t, k).wait_send()
        dk_out[...] = (rk[0].astype(F32) + rk[1].astype(F32)).astype(BF16)
        dv_out[...] = (rv[0].astype(F32) + rv[1].astype(F32)).astype(BF16)

    for t in range(2):
        for k in range(1, PEERS):
            kv_copy(k, t).wait_send()
    for part in range(SPLIT):
        for k in range(1, PEERS):
            in_copy(q_in, q, q_s, q_r, part, k).wait_send()
            in_copy(g_in, g, g_s, g_r, part, k).wait_send()
    for h in range(GROUP):
        dq_local(h).wait()
        for k in range(1, PEERS):
            dq_copy(h, k).wait()


def place(*refs):
    for source, target in zip(refs[:4], refs[4:]):
        target[...] = source[...]


def body(queries, keys, values, cotangent, readout, rewards, saved, ends, segs):
    vmem = pl.BlockSpec(memory_space=pltpu.VMEM)
    hbm = pl.BlockSpec(memory_space=pl.ANY)
    dma = pltpu.SemaphoreType.DMA
    grads = pl.pallas_call(
        kernel,
        out_shape=(
            jax.ShapeDtypeStruct(queries.shape, BF16),
            jax.ShapeDtypeStruct(keys.shape, BF16),
            jax.ShapeDtypeStruct(values.shape, BF16),
            jax.ShapeDtypeStruct((1, D), F32),
        ),
        in_specs=[hbm, hbm, hbm, hbm, vmem, vmem, vmem, vmem, vmem],
        out_specs=(hbm, vmem, vmem, vmem),
        scratch_shapes=[
            pltpu.VMEM((ROWS, ROWS), BF16),
            pltpu.VMEM((ROWS, ROWS), BF16),
            pltpu.VMEM((ROWS, ROWS), BF16),
            pltpu.VMEM((KEYS, 2 * D), BF16),
            pltpu.VMEM((KEYS, D), BF16),
            pltpu.VMEM((D, KEYS), BF16),
            pltpu.VMEM((D, KEYS), BF16),
            pltpu.VMEM((ROWS, D), BF16),
            pltpu.VMEM((GROUP, KEYS, ROWS), BF16),
            pltpu.VMEM((GROUP, D, ROWS), BF16),
            pltpu.VMEM((GROUP, D, ROWS), BF16),
            pltpu.VMEM((KEYS, ROWS), BF16),
            pltpu.VMEM((2, KEYS, T), F32),
            pltpu.VMEM((KEYS, D), F32),
            pltpu.VMEM((KEYS, D), F32),
            pltpu.VMEM((KEYS, D), BF16),
            pltpu.VMEM((KEYS, D), BF16),
            pltpu.VMEM((2, D, ROWS), BF16),
            pltpu.VMEM((2, D, ROWS), BF16),
            pltpu.VMEM((16, 8, D), F32),
            pltpu.VMEM((2, 8, D), F32),
            pltpu.VMEM((PEERS, D), F32),
            pltpu.VMEM((PEERS, PEERS, D), F32),
            pltpu.VMEM((GROUP, PEERS, D), F32),
            pltpu.VMEM((GROUP, D, D), F32),
            pltpu.VMEM((D, D), F32),
            pltpu.VMEM((HEADS, 8, ROWS), F32),
            dma((SPLIT, PEERS)), dma((SPLIT, PEERS)),
            dma((SPLIT, PEERS)), dma((SPLIT, PEERS)),
            dma((GROUP, PEERS)), dma((GROUP, PEERS)),
            dma((2, PEERS)), dma((2, PEERS)),
            dma((2, PEERS)), dma((2, PEERS)),
            dma((16,)), dma((16,)),
            dma, dma,
            dma((PEERS,)), dma((PEERS,)),
            dma((2, 2, PEERS)), dma((2, 2, PEERS)),
            dma((2,)),
        ],
        compiler_params=pltpu.CompilerParams(
            collective_id=0, has_side_effects=True, vmem_limit_bytes=62 << 20
        ),
    )(
        queries, keys, values, cotangent, readout.reshape(1, PEERS * GROUP * D),
        rewards.reshape(1, D), saved.reshape(1, D), ends.reshape(1, D), segs.reshape(1, D),
    )
    blocks = [pl.BlockSpec((D // 4, a.shape[1]), lambda i: (i, 0)) for a in grads[:3]]
    blocks.append(pl.BlockSpec((1, D), lambda i: (0, 0)))
    done = pl.pallas_call(
        place,
        grid=(4,),
        out_shape=[jax.ShapeDtypeStruct(a.shape, a.dtype) for a in grads],
        in_specs=blocks,
        out_specs=blocks,
    )(*grads)
    return (done[0], done[1], done[2], done[3].reshape(D))


def solution(mesh):
    rows, flat = P(("seq", "dp"), None), P(("seq", "dp"))
    return jax.shard_map(
        body,
        mesh=mesh,
        in_specs=(rows, rows, rows, rows, P(), flat, flat, flat, flat),
        out_specs=(rows, rows, rows, flat),
        check_vma=False,
    )
```

```python
import math

import jax
import jax.numpy as jnp
from jax import lax
from jax.experimental import pallas as pl
from jax.experimental.pallas import tpu as pltpu
from jax.sharding import PartitionSpec as P

MESH = pl.DeviceIdType.MESH
F32, BF16 = jnp.float32, jnp.bfloat16
D = 128
PEERS = 8
GROUP = 8
ROWS = PEERS * D
KEYS = 2 * ROWS
T = 256
NB = ROWS // T
STEP = 2
SPLIT = 4
HEADS = GROUP // SPLIT
WIDE = HEADS * D
BIG = 1e30
SCALE = 1.0 / math.sqrt(D)
EXP2 = SCALE * math.log2(math.e)


def mm(a, b, dims=((1,), (0,))):
    return lax.dot_general(a, b, (dims, ((), ())), preferred_element_type=F32)


def ds(start, size):
    if isinstance(start, int):
        return pl.ds(start, size)
    return pl.ds(pl.multiple_of(start, size), size)


def kernel(
    q_in, k_in, v_in, g_in, readout_in, rewards_in, saved_in, ends_in, segs_in,
    dq_out, dk_out, dv_out, adv_out,
    q, g, dq, kaug, v, kt, vt, qm, probs, ohi, olo, dsc, sc, dka, dva, dkb, dvb, rk, rv,
    pk, tot, est, es, inv, rcol, vet, rd,
    q_s, q_r, g_s, g_r, d_s, d_r, kv_s, kv_r, x_s, x_r, pk_s, pk_r, tot_s, tot_r, es_s, es_r, o_s, o_r, loc,
):
    me = lax.axis_index("dp")
    sq = lax.axis_index("seq")
    seqs = lax.axis_size("seq")
    x = lax.div(me, PEERS)
    hd = lax.rem(me, PEERS)
    late = x == 1

    def dev(half, place):
        return (half * PEERS + place, sq)

    def nxt(k):
        return lax.rem(hd + k, PEERS)

    def send(src, dst, ssem, rsem, device):
        return pltpu.make_async_remote_copy(
            src_ref=src, dst_ref=dst, send_sem=ssem, recv_sem=rsem, device_id=device, device_id_type=MESH
        )

    def readout_row(h):
        return readout_in[:, ds((hd * GROUP + h) * D, D)]

    barrier = pltpu.get_barrier_semaphore()
    for k in range(1, 16):
        pl.semaphore_signal(barrier, inc=1, device_id=(lax.rem(me + k, 16), sq), device_id_type=MESH)
    for k in (1, seqs - 1):
        pl.semaphore_signal(barrier, inc=1, device_id=(me, lax.rem(sq + k, seqs)), device_id_type=MESH)

    def kv_copy(k, t):
        src, dst = ((k_in, kaug), (v_in, v))[t]
        p = nxt(k)
        return send(
            src.at[:, ds(p * D, D)], dst.at[ds(ROWS + hd * D, D), pl.ds(0, D)], kv_s.at[t, k], kv_r.at[t, k], dev(x, p)
        )

    def kv_local(t):
        src, dst = ((k_in, kaug), (v_in, v))[t]
        return pltpu.make_async_copy(src.at[:, ds(hd * D, D)], dst.at[ds(ROWS + hd * D, D), pl.ds(0, D)], kv_r.at[t, 0])

    def in_copy(src, dst, ssem, rsem, part, k):
        p = nxt(k)
        return send(
            src.at[:, ds((p * SPLIT + part) * WIDE, WIDE)],
            dst.at[ds(hd * D, D), ds(part * WIDE, WIDE)],
            ssem.at[part, k], rsem.at[part, k], dev(x, p),
        )

    def in_local(src, dst, rsem, part):
        return pltpu.make_async_copy(
            src.at[:, ds((hd * SPLIT + part) * WIDE, WIDE)], dst.at[ds(hd * D, D), ds(part * WIDE, WIDE)], rsem.at[part, 0]
        )

    def start_in(src, dst, ssem, rsem, part):
        in_local(src, dst, rsem, part).start()
        for k in range(1, PEERS):
            in_copy(src, dst, ssem, rsem, part, k).start()

    def wait_in(src, dst, ssem, rsem, part):
        in_local(src, dst, rsem, part).wait()
        for k in range(1, PEERS):
            in_copy(src, dst, ssem, rsem, part, k).wait_recv()

    def x_copy(t, k):
        src, dst = ((k_in, kaug), (v_in, v))[t]
        p = nxt(k)
        return send(
            src.at[:, ds(p * D, D)], dst.at[ds(hd * D, D), pl.ds(0, D)], x_s.at[t, k], x_r.at[t, k], dev(1 - x, p)
        )

    sub = lax.broadcasted_iota(jnp.int32, (D, D), 0)
    lane = lax.broadcasted_iota(jnp.int32, (D, D), 1)
    lane_f = lane.astype(F32)

    def wide(row):
        return jnp.broadcast_to(row, (D, D))

    def column(row):
        return wide(row).T

    last = jnp.logical_and(me == 15, jnp.logical_or(sq == seqs // 2 - 1, sq == seqs - 1))
    ends = ends_in[...].astype(F32)
    row_lane = lax.broadcasted_iota(jnp.int32, (1, D), 1)
    ends = jnp.where(jnp.logical_and(row_lane == D - 1, last), 1.0, ends)
    ends_col = column(ends)
    before = jnp.sum(jnp.where(sub < lane, ends_col, 0.0), axis=0, keepdims=True)
    total_ends = jnp.sum(ends, axis=1, keepdims=True)
    reach = jnp.logical_and(sub >= lane, column(before) == wide(before))
    local_gain = jnp.sum(jnp.where(reach, column(rewards_in[...]), 0.0), axis=0, keepdims=True)
    passing = (total_ends - before == 0).astype(F32)
    through = (total_ends == 0).astype(F32)
    pk[me, 0:1, :] = segs_in[...].astype(F32)
    pk[me, 1:2, :] = jnp.broadcast_to(through, (1, D))
    pk[me, 2:3, :] = jnp.broadcast_to(local_gain[:, 0:1], (1, D))

    def pk_copy(k):
        return send(pk.at[me], pk.at[me], pk_s.at[k], pk_r.at[k], (lax.rem(me + k, 16), sq))

    pl.semaphore_wait(barrier, 17)
    for k in range(1, 16):
        pk_copy(k).start()
    @pl.when(x == 0)
    def _():
        for t in range(2):
            for k in range(PEERS):
                x_copy(t, k).start()

    for t in range(2):
        kv_local(t).start()
        for k in range(1, PEERS):
            kv_copy(k, t).start()


    for part in range(SPLIT):
        start_in(q_in, q, q_s, q_r, part)

    @pl.when(x == 0)
    def _():
        kaug[0:ROWS, 0:D] = jnp.zeros((ROWS, D), BF16)
        v[0:ROWS, :] = jnp.zeros((ROWS, D), BF16)

    for h in range(GROUP):
        rcol[h] = column(readout_row(h))
    est[...] = jnp.zeros_like(est)
    dka[...] = jnp.zeros_like(dka)
    dva[...] = jnp.zeros_like(dva)

    for k in range(1, 16):
        pk_copy(k).wait()

    def fold(value, lowest):
        for d in range(15, -1, -1):
            joined = pk[d, 2:3, :] + pk[d, 1:2, :] * value
            value = joined if lowest is None else jnp.where(d >= lowest, joined, value)
        return value

    tot[0] = jnp.broadcast_to(fold(jnp.zeros((1, D), F32), None), (8, D))
    tot_copy = send(tot.at[0], tot.at[1], tot_s, tot_r, (me, lax.rem(sq + seqs - 1, seqs)))
    tot_copy.start()

    lines = [pk[(1 - x) * PEERS + b, 0:1, :] for b in range(PEERS)] + [pk[x * PEERS + b, 0:1, :] for b in range(PEERS)]
    codes = (jnp.concatenate(lines * (D // 16), axis=0) - pk[0, 0:1, 0:1]).T
    for b in range(2 * PEERS):
        code = jnp.broadcast_to(codes[:, b : b + 1], (D, D))
        if b < PEERS:
            code = jnp.where(x == 0, 100.0, code)
        else:
            qm[(b - PEERS) * D : (b - PEERS + 1) * D, :] = jnp.where(code == lane_f, 0.0, -BIG).astype(BF16)
        kaug[b * D : (b + 1) * D, D : 2 * D] = jnp.where(code == lane_f, 1.0, 0.0).astype(BF16)

    for t in range(2):
        kv_local(t).wait()
        for k in range(1, PEERS):
            kv_copy(k, t).wait_recv()

    @pl.when(late)
    def _():
        for t in range(2):
            for k in range(PEERS):
                x_copy(t, k).wait_recv()

    for b in range(2 * PEERS):
        vt[:, b * D : (b + 1) * D] = v[b * D : (b + 1) * D, :].T

    tile_sub = lax.broadcasted_iota(jnp.int32, (T, T), 0)
    tile_lane = lax.broadcasted_iota(jnp.int32, (T, T), 1)

    def forward(heads):
        steps = [(h, i) for h in heads for i in range(NB)]
        state = {}

        def score(t, j, to):
            h, i = steps[t]
            cols, r = ds(h * D, D), slice(i * T, (i + 1) * T)
            if j == 0:
                state["q", t] = jnp.concatenate([q[r, cols], qm[r, :]], axis=1)
            s = mm(kaug[j * T : to * T, :], state["q", t], ((1,), (1,)))
            if to == NB + i + 1:
                own = jnp.where(tile_sub <= tile_lane, s[(to - 1 - j) * T :, :], -BIG)
                s = own if to == j + 1 else jnp.concatenate([s[: (to - 1 - j) * T, :], own], axis=0)
            sc[t % 2, j * T : to * T, :] = s
            part = jnp.max(s.reshape((to - j) * T // 8, 8, T), axis=0)
            state["top", t] = part if j == 0 else jnp.maximum(state["top", t], part)
            if to == NB + i + 1:
                state["top", t] = jnp.max(state["top", t], axis=0, keepdims=True) * EXP2

        def weigh(t, j, to):
            h, i = steps[t]
            r = slice(i * T, (i + 1) * T)
            p = jnp.exp2(sc[t % 2, j * T : to * T, :] * EXP2 - state["top", t])
            part = jnp.sum(p.reshape((to - j) * T // 8, 8, T), axis=0)
            state["sum", t] = part if j == 0 else state["sum", t] + part
            probs[h, j * T : to * T, r] = p.astype(BF16)

        def output(t):
            h, i = steps[t]
            r, n = slice(i * T, (i + 1) * T), (NB + i + 1) * T
            scale = 1.0 / jnp.sum(state["sum", t], axis=0, keepdims=True)
            out = mm(vt[:, 0:n], probs[h, 0:n, r]) * scale
            high = out.astype(BF16)
            ohi[h, :, r] = high
            olo[h, :, r] = (out - high.astype(F32)).astype(BF16)
            for c in range(T // D):
                b = i * (T // D) + c
                half = slice(c * D, (c + 1) * D)
                est[b : b + 1, :] += jnp.sum(out[:, half] * rcol[h], axis=0, keepdims=True)
                inv[h, b : b + 1, :] = scale[:, half]

        for t in range(len(steps) + 2):
            if t >= 2:
                output(t - 2)
            for j in range(0, 2 * NB, STEP):
                if t < len(steps) and j <= NB + steps[t][1]:
                    score(t, j, min(j + STEP, NB + steps[t][1] + 1))
                if 1 <= t <= len(steps) and j <= NB + steps[t - 1][1]:
                    weigh(t - 1, j, min(j + STEP, NB + steps[t - 1][1] + 1))

    def forward_part(part, carry):
        wait_in(q_in, q, q_s, q_r, part)

        @pl.when(part >= 2)
        def _():
            start_in(g_in, g, g_s, g_r, part - 2)

        forward([part * HEADS + n for n in range(HEADS)])
        return carry

    lax.fori_loop(0, SPLIT, forward_part, 0)

    tot_copy.wait()
    beyond = tot[1, 0:1, :]
    gains = local_gain + passing * fold(beyond, me + 1)
    adv_out[...] = gains - saved_in[...]
    place_sub = lax.broadcasted_iota(jnp.int32, (PEERS, D), 0)
    es[hd] = est[...] - jnp.where(place_sub == hd, jnp.broadcast_to(gains, (PEERS, D)), 0.0)

    def es_copy(k):
        return send(es.at[hd], es.at[hd], es_s.at[k], es_r.at[k], dev(x, nxt(k)))

    for k in range(1, PEERS):
        es_copy(k).start()
    for part in range(SPLIT - 2, SPLIT):
        start_in(g_in, g, g_s, g_r, part)
    for b in range(2 * PEERS):
        kt[:, b * D : (b + 1) * D] = kaug[b * D : (b + 1) * D, 0:D].T
    for k in range(1, PEERS):
        es_copy(k).wait()
    error = es[0]
    for d in range(1, PEERS):
        error = error + es[d]
    vet[...] = jnp.concatenate([error] * (D // PEERS), axis=0).T

    def prepare(n, h):
        cols = ds(h * D, D)
        scales = jnp.concatenate([inv[h]] * (D // PEERS), axis=0).T
        readout = readout_row(h)

        def block(b):
            r = slice(b * D, (b + 1) * D)
            grad = g[r, cols].astype(F32) + vet[:, b : b + 1] * readout
            grad = (grad * scales[:, b : b + 1]).astype(BF16)
            g[r, cols] = grad
            cross = mm(grad, ohi[h, :, r]) + mm(grad, olo[h, :, r])
            rd[n, :, r] = jnp.broadcast_to(jnp.sum(jnp.where(sub == lane, cross, 0.0), axis=0, keepdims=True), (8, D))

        return [(block, (b,)) for b in range(PEERS)]

    def units(n, h, own):
        cols = ds(h * D, D)
        base = ROWS if own else 0

        def grads(i, j, to):
            r, a = slice(i * T, (i + 1) * T), slice(base + j * T, base + to * T)
            c = slice(n * ROWS + j * T, n * ROWS + to * T)
            dp = mm(v[a, :], g[r, cols], ((1,), (1,)))
            dsc[c, r] = (probs[h, a, r].astype(F32) * (dp - rd[n, 0:1, r])).astype(BF16)
            count = i + 1 if own else NB
            if to == count:
                out = mm(kt[:, base : base + count * T], dsc[n * ROWS : n * ROWS + count * T, r])
                keep = slice(i * D, (i + 1) * D)
                if own:
                    dq[r, cols] = ((sc[n, keep, :] + out) * SCALE).T.astype(BF16)
                else:
                    sc[n, keep, :] = out

        def value(j):
            a, low = slice(base + j * T, base + (j + 1) * T), j * T if own else 0
            dva[a, :] += mm(probs[h, a, low:ROWS], g[low:ROWS, cols])

        def key(j):
            a, low = slice(base + j * T, base + (j + 1) * T), j * T if own else 0
            c = slice(n * ROWS + j * T, n * ROWS + (j + 1) * T)
            dka[a, :] += mm(dsc[c, low:ROWS], q[low:ROWS, cols])

        first = [
            (grads, (i, j, min(j + STEP, count)))
            for i, count in enumerate(range(1, NB + 1) if own else [NB] * NB)
            for j in range(0, count, STEP)
        ]
        return first, [(value, (j,)) for j in range(NB)], [(key, (j,)) for j in range(NB)]

    def blend(long, short):
        taken = 0
        for index, (unit, arg) in enumerate(long):
            unit(*arg)
            while taken < len(short) and taken * len(long) < (index + 1) * len(short):
                short[taken][0](*short[taken][1])
                taken += 1

    def dq_copy(h, k):
        p = nxt(k)
        return send(
            dq.at[ds(p * D, D), ds(h * D, D)], dq_out.at[:, ds((hd * GROUP + h) * D, D)], d_s.at[h, k], d_r.at[h, k], dev(x, p)
        )

    def dq_local(h):
        return pltpu.make_async_copy(
            dq.at[ds(hd * D, D), ds(h * D, D)], dq_out.at[:, ds((hd * GROUP + h) * D, D)], d_r.at[h, 0]
        )

    def run(list_of_units):
        for unit, arg in list_of_units:
            unit(*arg)

    def backward_half(heads, own):
        if not own:
            run(prepare(0, heads[0]))
        pending = []
        for n, h in enumerate(heads):
            first, values, keys = units(n, h, own)
            ahead = prepare(n + 1, heads[n + 1]) if not own and n + 1 < len(heads) else []
            blend(first, ahead + values + pending)
            pending = keys
            if own:
                dq_local(h).start()
                for k in range(1, PEERS):
                    dq_copy(h, k).start()
        return pending

    def out_copy(t, k, same):
        src, dst = ((dkb, rk), (dvb, rv))[t]
        p, slot = nxt(k), 1 if same else 0
        return send(
            src.at[ds(slot * ROWS + p * D, D), :], dst.at[slot, :, ds(hd * D, D)],
            o_s.at[t, slot, k], o_r.at[t, slot, k], dev(x if same else 1 - x, p),
        )

    def backward_part(part, carry):
        wait_in(g_in, g, g_s, g_r, part)
        heads = [part * HEADS + n for n in range(HEADS)]
        run(backward_half(heads, False))

        @pl.when(jnp.logical_and(late, part == SPLIT - 1))
        def _():
            dkb[0:ROWS, :] = (dka[0:ROWS, :] * SCALE).astype(BF16)
            dvb[0:ROWS, :] = dva[0:ROWS, :].astype(BF16)
            for t in range(2):
                for k in range(PEERS):
                    out_copy(t, k, False).start()

        run(backward_half(heads, True))
        return carry

    lax.fori_loop(0, SPLIT, backward_part, 0)

    dkb[ROWS:KEYS, :] = (dka[ROWS:KEYS, :] * SCALE).astype(BF16)
    dvb[ROWS:KEYS, :] = dva[ROWS:KEYS, :].astype(BF16)

    def out_local(t):
        src, dst = ((dkb, rk), (dvb, rv))[t]
        return pltpu.make_async_copy(src.at[ds(ROWS + hd * D, D), :], dst.at[1, :, ds(hd * D, D)], loc.at[t])

    for t in range(2):
        out_local(t).start()
        for k in range(1, PEERS):
            out_copy(t, k, True).start()
    for t in range(2):
        out_local(t).wait()
        for k in range(1, PEERS):
            out_copy(t, k, True).wait()

    @pl.when(late)
    def _():
        for t in range(2):
            for k in range(PEERS):
                out_copy(t, k, False).wait_send()
        dk_out[...] = rk[1]
        dv_out[...] = rv[1]

    @pl.when(x == 0)
    def _():
        for t in range(2):
            for k in range(PEERS):
                out_copy(t, k, False).wait_recv()
                x_copy(t, k).wait_send()
        dk_out[...] = (rk[0].astype(F32) + rk[1].astype(F32)).astype(BF16)
        dv_out[...] = (rv[0].astype(F32) + rv[1].astype(F32)).astype(BF16)

    for t in range(2):
        for k in range(1, PEERS):
            kv_copy(k, t).wait_send()
    for part in range(SPLIT):
        for k in range(1, PEERS):
            in_copy(q_in, q, q_s, q_r, part, k).wait_send()
            in_copy(g_in, g, g_s, g_r, part, k).wait_send()
    for h in range(GROUP):
        dq_local(h).wait()
        for k in range(1, PEERS):
            dq_copy(h, k).wait()


def place(*refs):
    for source, target in zip(refs[:4], refs[4:]):
        target[...] = source[...]


def body(queries, keys, values, cotangent, readout, rewards, saved, ends, segs):
    vmem = pl.BlockSpec(memory_space=pltpu.VMEM)
    hbm = pl.BlockSpec(memory_space=pl.ANY)
    dma = pltpu.SemaphoreType.DMA
    grads = pl.pallas_call(
        kernel,
        out_shape=(
            jax.ShapeDtypeStruct(queries.shape, BF16),
            jax.ShapeDtypeStruct(keys.shape, BF16),
            jax.ShapeDtypeStruct(values.shape, BF16),
            jax.ShapeDtypeStruct((1, D), F32),
        ),
        in_specs=[hbm, hbm, hbm, hbm, vmem, vmem, vmem, vmem, vmem],
        out_specs=(hbm, vmem, vmem, vmem),
        scratch_shapes=[
            pltpu.VMEM((ROWS, ROWS), BF16),
            pltpu.VMEM((ROWS, ROWS), BF16),
            pltpu.VMEM((ROWS, ROWS), BF16),
            pltpu.VMEM((KEYS, 2 * D), BF16),
            pltpu.VMEM((KEYS, D), BF16),
            pltpu.VMEM((D, KEYS), BF16),
            pltpu.VMEM((D, KEYS), BF16),
            pltpu.VMEM((ROWS, D), BF16),
            pltpu.VMEM((GROUP, KEYS, ROWS), BF16),
            pltpu.VMEM((GROUP, D, ROWS), BF16),
            pltpu.VMEM((GROUP, D, ROWS), BF16),
            pltpu.VMEM((KEYS, ROWS), BF16),
            pltpu.VMEM((2, KEYS, T), F32),
            pltpu.VMEM((KEYS, D), F32),
            pltpu.VMEM((KEYS, D), F32),
            pltpu.VMEM((KEYS, D), BF16),
            pltpu.VMEM((KEYS, D), BF16),
            pltpu.VMEM((2, D, ROWS), BF16),
            pltpu.VMEM((2, D, ROWS), BF16),
            pltpu.VMEM((16, 8, D), F32),
            pltpu.VMEM((2, 8, D), F32),
            pltpu.VMEM((PEERS, D), F32),
            pltpu.VMEM((PEERS, PEERS, D), F32),
            pltpu.VMEM((GROUP, PEERS, D), F32),
            pltpu.VMEM((GROUP, D, D), F32),
            pltpu.VMEM((D, D), F32),
            pltpu.VMEM((HEADS, 8, ROWS), F32),
            dma((SPLIT, PEERS)), dma((SPLIT, PEERS)),
            dma((SPLIT, PEERS)), dma((SPLIT, PEERS)),
            dma((GROUP, PEERS)), dma((GROUP, PEERS)),
            dma((2, PEERS)), dma((2, PEERS)),
            dma((2, PEERS)), dma((2, PEERS)),
            dma((16,)), dma((16,)),
            dma, dma,
            dma((PEERS,)), dma((PEERS,)),
            dma((2, 2, PEERS)), dma((2, 2, PEERS)),
            dma((2,)),
        ],
        compiler_params=pltpu.CompilerParams(
            collective_id=0, has_side_effects=True, vmem_limit_bytes=62 << 20
        ),
    )(
        queries, keys, values, cotangent, readout.astype(F32).reshape(1, PEERS * GROUP * D),
        rewards.reshape(1, D), saved.reshape(1, D), ends.reshape(1, D), segs.reshape(1, D),
    )
    blocks = [pl.BlockSpec((D // 4, a.shape[1]), lambda i: (i, 0)) for a in grads[:3]]
    blocks.append(pl.BlockSpec((1, D), lambda i: (0, 0)))
    done = pl.pallas_call(
        place,
        grid=(4,),
        out_shape=[jax.ShapeDtypeStruct(a.shape, a.dtype) for a in grads],
        in_specs=blocks,
        out_specs=blocks,
    )(*grads)
    return (done[0], done[1], done[2], done[3].reshape(D))


def solution(mesh):
    rows, flat = P(("seq", "dp"), None), P(("seq", "dp"))
    return jax.shard_map(
        body,
        mesh=mesh,
        in_specs=(rows, rows, rows, rows, P(), flat, flat, flat, flat),
        out_specs=(rows, rows, rows, flat),
        check_vma=False,
    )
```

```python
import math

import jax
import jax.numpy as jnp
from jax import lax
from jax.experimental import pallas as pl
from jax.experimental.pallas import tpu as pltpu
from jax.sharding import PartitionSpec as P

MESH = pl.DeviceIdType.MESH
F32, BF16 = jnp.float32, jnp.bfloat16
D = 128
PEERS = 8
GROUP = 8
ROWS = PEERS * D
KEYS = 2 * ROWS
T = 256
NB = ROWS // T
STEP = 2
SPLIT = 8
HEADS = GROUP // SPLIT
WIDE = HEADS * D
BIG = 1e30
SCALE = 1.0 / math.sqrt(D)
EXP2 = SCALE * math.log2(math.e)


def mm(a, b, dims=((1,), (0,))):
    return lax.dot_general(a, b, (dims, ((), ())), preferred_element_type=F32)


def ds(start, size):
    if isinstance(start, int):
        return pl.ds(start, size)
    return pl.ds(pl.multiple_of(start, size), size)


def kernel(
    q_in, k_in, v_in, g_in, readout_in, rewards_in, saved_in, ends_in, segs_in,
    dq_out, dk_out, dv_out, adv_out,
    q, g, dq, kaug, v, kt, vt, qm, probs, ohi, olo, dsc, sc, dka, dva, dkb, dvb, rk, rv,
    pk, tot, est, es, inv, rcol, vet, rd,
    q_s, q_r, g_s, g_r, d_s, d_r, kv_s, kv_r, x_s, x_r, pk_s, pk_r, tot_s, tot_r, es_s, es_r, o_s, o_r, loc,
):
    me = lax.axis_index("dp")
    sq = lax.axis_index("seq")
    seqs = lax.axis_size("seq")
    x = lax.div(me, PEERS)
    hd = lax.rem(me, PEERS)
    late = x == 1

    def dev(half, place):
        return (half * PEERS + place, sq)

    def nxt(k):
        return lax.rem(hd + k, PEERS)

    def send(src, dst, ssem, rsem, device):
        return pltpu.make_async_remote_copy(
            src_ref=src, dst_ref=dst, send_sem=ssem, recv_sem=rsem, device_id=device, device_id_type=MESH
        )

    def readout_row(h):
        return readout_in[:, ds((hd * GROUP + h) * D, D)]

    barrier = pltpu.get_barrier_semaphore()
    for k in range(1, 16):
        pl.semaphore_signal(barrier, inc=1, device_id=(lax.rem(me + k, 16), sq), device_id_type=MESH)
    for k in (1, seqs - 1):
        pl.semaphore_signal(barrier, inc=1, device_id=(me, lax.rem(sq + k, seqs)), device_id_type=MESH)

    def kv_copy(k, t):
        src, dst = ((k_in, kaug), (v_in, v))[t]
        p = nxt(k)
        return send(
            src.at[:, ds(p * D, D)], dst.at[ds(ROWS + hd * D, D), pl.ds(0, D)], kv_s.at[t, k], kv_r.at[t, k], dev(x, p)
        )

    def kv_local(t):
        src, dst = ((k_in, kaug), (v_in, v))[t]
        return pltpu.make_async_copy(src.at[:, ds(hd * D, D)], dst.at[ds(ROWS + hd * D, D), pl.ds(0, D)], kv_r.at[t, 0])

    def in_copy(src, dst, ssem, rsem, part, k):
        p = nxt(k)
        return send(
            src.at[:, ds((p * SPLIT + part) * WIDE, WIDE)],
            dst.at[ds(hd * D, D), ds(part * WIDE, WIDE)],
            ssem.at[part, k], rsem.at[part, k], dev(x, p),
        )

    def in_local(src, dst, rsem, part):
        return pltpu.make_async_copy(
            src.at[:, ds((hd * SPLIT + part) * WIDE, WIDE)], dst.at[ds(hd * D, D), ds(part * WIDE, WIDE)], rsem.at[part, 0]
        )

    def start_in(src, dst, ssem, rsem, part):
        in_local(src, dst, rsem, part).start()
        for k in range(1, PEERS):
            in_copy(src, dst, ssem, rsem, part, k).start()

    def wait_in(src, dst, ssem, rsem, part):
        in_local(src, dst, rsem, part).wait()
        for k in range(1, PEERS):
            in_copy(src, dst, ssem, rsem, part, k).wait_recv()

    def x_copy(t, k):
        src, dst = ((k_in, kaug), (v_in, v))[t]
        p = nxt(k)
        return send(
            src.at[:, ds(p * D, D)], dst.at[ds(hd * D, D), pl.ds(0, D)], x_s.at[t, k], x_r.at[t, k], dev(1 - x, p)
        )

    sub = lax.broadcasted_iota(jnp.int32, (D, D), 0)
    lane = lax.broadcasted_iota(jnp.int32, (D, D), 1)
    lane_f = lane.astype(F32)

    def wide(row):
        return jnp.broadcast_to(row, (D, D))

    def column(row):
        return wide(row).T

    last = jnp.logical_and(me == 15, jnp.logical_or(sq == seqs // 2 - 1, sq == seqs - 1))
    ends = ends_in[...].astype(F32)
    row_lane = lax.broadcasted_iota(jnp.int32, (1, D), 1)
    ends = jnp.where(jnp.logical_and(row_lane == D - 1, last), 1.0, ends)
    ends_col = column(ends)
    before = jnp.sum(jnp.where(sub < lane, ends_col, 0.0), axis=0, keepdims=True)
    total_ends = jnp.sum(ends, axis=1, keepdims=True)
    reach = jnp.logical_and(sub >= lane, column(before) == wide(before))
    local_gain = jnp.sum(jnp.where(reach, column(rewards_in[...]), 0.0), axis=0, keepdims=True)
    passing = (total_ends - before == 0).astype(F32)
    through = (total_ends == 0).astype(F32)
    pk[me, 0:1, :] = segs_in[...].astype(F32)
    pk[me, 1:2, :] = jnp.broadcast_to(through, (1, D))
    pk[me, 2:3, :] = jnp.broadcast_to(local_gain[:, 0:1], (1, D))

    def pk_copy(k):
        return send(pk.at[me], pk.at[me], pk_s.at[k], pk_r.at[k], (lax.rem(me + k, 16), sq))

    pl.semaphore_wait(barrier, 17)
    for k in range(1, 16):
        pk_copy(k).start()
    @pl.when(x == 0)
    def _():
        for t in range(2):
            for k in range(PEERS):
                x_copy(t, k).start()

    for t in range(2):
        kv_local(t).start()
        for k in range(1, PEERS):
            kv_copy(k, t).start()


    for part in range(SPLIT):
        start_in(q_in, q, q_s, q_r, part)

    @pl.when(x == 0)
    def _():
        kaug[0:ROWS, 0:D] = jnp.zeros((ROWS, D), BF16)
        v[0:ROWS, :] = jnp.zeros((ROWS, D), BF16)

    for h in range(GROUP):
        rcol[h] = column(readout_row(h))
    est[...] = jnp.zeros_like(est)
    dka[...] = jnp.zeros_like(dka)
    dva[...] = jnp.zeros_like(dva)

    for k in range(1, 16):
        pk_copy(k).wait()

    def fold(value, lowest):
        for d in range(15, -1, -1):
            joined = pk[d, 2:3, :] + pk[d, 1:2, :] * value
            value = joined if lowest is None else jnp.where(d >= lowest, joined, value)
        return value

    tot[0] = jnp.broadcast_to(fold(jnp.zeros((1, D), F32), None), (8, D))
    tot_copy = send(tot.at[0], tot.at[1], tot_s, tot_r, (me, lax.rem(sq + seqs - 1, seqs)))
    tot_copy.start()

    lines = [pk[(1 - x) * PEERS + b, 0:1, :] for b in range(PEERS)] + [pk[x * PEERS + b, 0:1, :] for b in range(PEERS)]
    codes = (jnp.concatenate(lines * (D // 16), axis=0) - pk[0, 0:1, 0:1]).T
    for b in range(2 * PEERS):
        code = jnp.broadcast_to(codes[:, b : b + 1], (D, D))
        if b < PEERS:
            code = jnp.where(x == 0, 100.0, code)
        else:
            qm[(b - PEERS) * D : (b - PEERS + 1) * D, :] = jnp.where(code == lane_f, 0.0, -BIG).astype(BF16)
        kaug[b * D : (b + 1) * D, D : 2 * D] = jnp.where(code == lane_f, 1.0, 0.0).astype(BF16)

    for t in range(2):
        kv_local(t).wait()
        for k in range(1, PEERS):
            kv_copy(k, t).wait_recv()

    @pl.when(late)
    def _():
        for t in range(2):
            for k in range(PEERS):
                x_copy(t, k).wait_recv()

    for b in range(2 * PEERS):
        vt[:, b * D : (b + 1) * D] = v[b * D : (b + 1) * D, :].T

    tile_sub = lax.broadcasted_iota(jnp.int32, (T, T), 0)
    tile_lane = lax.broadcasted_iota(jnp.int32, (T, T), 1)

    def forward(heads):
        steps = [(h, i) for h in heads for i in range(NB)]
        state = {}

        def score(t, j, to):
            h, i = steps[t]
            cols, r = ds(h * D, D), slice(i * T, (i + 1) * T)
            if j == 0:
                state["q", t] = jnp.concatenate([q[r, cols], qm[r, :]], axis=1)
            s = mm(kaug[j * T : to * T, :], state["q", t], ((1,), (1,)))
            if to == NB + i + 1:
                own = jnp.where(tile_sub <= tile_lane, s[(to - 1 - j) * T :, :], -BIG)
                s = own if to == j + 1 else jnp.concatenate([s[: (to - 1 - j) * T, :], own], axis=0)
            sc[t % 2, j * T : to * T, :] = s
            part = jnp.max(s.reshape((to - j) * T // 8, 8, T), axis=0)
            state["top", t] = part if j == 0 else jnp.maximum(state["top", t], part)
            if to == NB + i + 1:
                state["top", t] = jnp.max(state["top", t], axis=0, keepdims=True) * EXP2

        def weigh(t, j, to):
            h, i = steps[t]
            r = slice(i * T, (i + 1) * T)
            p = jnp.exp2(sc[t % 2, j * T : to * T, :] * EXP2 - state["top", t])
            part = jnp.sum(p.reshape((to - j) * T // 8, 8, T), axis=0)
            state["sum", t] = part if j == 0 else state["sum", t] + part
            probs[h, j * T : to * T, r] = p.astype(BF16)

        def output(t):
            h, i = steps[t]
            r, n = slice(i * T, (i + 1) * T), (NB + i + 1) * T
            scale = 1.0 / jnp.sum(state["sum", t], axis=0, keepdims=True)
            out = mm(vt[:, 0:n], probs[h, 0:n, r]) * scale
            high = out.astype(BF16)
            ohi[h, :, r] = high
            olo[h, :, r] = (out - high.astype(F32)).astype(BF16)
            for c in range(T // D):
                b = i * (T // D) + c
                half = slice(c * D, (c + 1) * D)
                est[b : b + 1, :] += jnp.sum(out[:, half] * rcol[h], axis=0, keepdims=True)
                inv[h, b : b + 1, :] = scale[:, half]

        for t in range(len(steps) + 2):
            if t >= 2:
                output(t - 2)
            for j in range(0, 2 * NB, STEP):
                if t < len(steps) and j <= NB + steps[t][1]:
                    score(t, j, min(j + STEP, NB + steps[t][1] + 1))
                if 1 <= t <= len(steps) and j <= NB + steps[t - 1][1]:
                    weigh(t - 1, j, min(j + STEP, NB + steps[t - 1][1] + 1))

    def forward_part(part, carry):
        wait_in(q_in, q, q_s, q_r, part)

        @pl.when(part >= SPLIT // 2)
        def _():
            start_in(g_in, g, g_s, g_r, part - SPLIT // 2)

        forward([part * HEADS + n for n in range(HEADS)])
        return carry

    lax.fori_loop(0, SPLIT, forward_part, 0)

    tot_copy.wait()
    beyond = tot[1, 0:1, :]
    gains = local_gain + passing * fold(beyond, me + 1)
    adv_out[...] = gains - saved_in[...]
    place_sub = lax.broadcasted_iota(jnp.int32, (PEERS, D), 0)
    es[hd] = est[...] - jnp.where(place_sub == hd, jnp.broadcast_to(gains, (PEERS, D)), 0.0)

    def es_copy(k):
        return send(es.at[hd], es.at[hd], es_s.at[k], es_r.at[k], dev(x, nxt(k)))

    for k in range(1, PEERS):
        es_copy(k).start()
    for part in range(SPLIT // 2, SPLIT):
        start_in(g_in, g, g_s, g_r, part)
    for b in range(2 * PEERS):
        kt[:, b * D : (b + 1) * D] = kaug[b * D : (b + 1) * D, 0:D].T
    for k in range(1, PEERS):
        es_copy(k).wait()
    error = es[0]
    for d in range(1, PEERS):
        error = error + es[d]
    vet[...] = jnp.concatenate([error] * (D // PEERS), axis=0).T

    def prepare(n, h):
        cols = ds(h * D, D)
        scales = jnp.concatenate([inv[h]] * (D // PEERS), axis=0).T
        readout = readout_row(h)

        def block(b):
            r = slice(b * D, (b + 1) * D)
            grad = g[r, cols].astype(F32) + vet[:, b : b + 1] * readout
            grad = (grad * scales[:, b : b + 1]).astype(BF16)
            g[r, cols] = grad
            cross = mm(grad, ohi[h, :, r]) + mm(grad, olo[h, :, r])
            rd[n, :, r] = jnp.broadcast_to(jnp.sum(jnp.where(sub == lane, cross, 0.0), axis=0, keepdims=True), (8, D))

        return [(block, (b,)) for b in range(PEERS)]

    def units(n, h, own):
        cols = ds(h * D, D)
        base = ROWS if own else 0

        def grads(i, j, to):
            r, a = slice(i * T, (i + 1) * T), slice(base + j * T, base + to * T)
            c = slice(n * ROWS + j * T, n * ROWS + to * T)
            dp = mm(v[a, :], g[r, cols], ((1,), (1,)))
            dsc[c, r] = (probs[h, a, r].astype(F32) * (dp - rd[n, 0:1, r])).astype(BF16)
            count = i + 1 if own else NB
            if to == count:
                out = mm(kt[:, base : base + count * T], dsc[n * ROWS : n * ROWS + count * T, r])
                keep = slice(i * D, (i + 1) * D)
                if own:
                    dq[r, cols] = ((sc[n, keep, :] + out) * SCALE).T.astype(BF16)
                else:
                    sc[n, keep, :] = out

        def value(j):
            a, low = slice(base + j * T, base + (j + 1) * T), j * T if own else 0
            dva[a, :] += mm(probs[h, a, low:ROWS], g[low:ROWS, cols])

        def key(j):
            a, low = slice(base + j * T, base + (j + 1) * T), j * T if own else 0
            c = slice(n * ROWS + j * T, n * ROWS + (j + 1) * T)
            dka[a, :] += mm(dsc[c, low:ROWS], q[low:ROWS, cols])

        first = [
            (grads, (i, j, min(j + STEP, count)))
            for i, count in enumerate(range(1, NB + 1) if own else [NB] * NB)
            for j in range(0, count, STEP)
        ]
        return first, [(value, (j,)) for j in range(NB)], [(key, (j,)) for j in range(NB)]

    def blend(long, short):
        taken = 0
        for index, (unit, arg) in enumerate(long):
            unit(*arg)
            while taken < len(short) and taken * len(long) < (index + 1) * len(short):
                short[taken][0](*short[taken][1])
                taken += 1

    def dq_copy(h, k):
        p = nxt(k)
        return send(
            dq.at[ds(p * D, D), ds(h * D, D)], dq_out.at[:, ds((hd * GROUP + h) * D, D)], d_s.at[h, k], d_r.at[h, k], dev(x, p)
        )

    def dq_local(h):
        return pltpu.make_async_copy(
            dq.at[ds(hd * D, D), ds(h * D, D)], dq_out.at[:, ds((hd * GROUP + h) * D, D)], d_r.at[h, 0]
        )

    def run(list_of_units):
        for unit, arg in list_of_units:
            unit(*arg)

    def backward_half(heads, own):
        if not own:
            run(prepare(0, heads[0]))
        pending = []
        for n, h in enumerate(heads):
            first, values, keys = units(n, h, own)
            ahead = prepare(n + 1, heads[n + 1]) if not own and n + 1 < len(heads) else []
            blend(first, ahead + values + pending)
            pending = keys
            if own:
                dq_local(h).start()
                for k in range(1, PEERS):
                    dq_copy(h, k).start()
        return pending

    def out_copy(t, k, same):
        src, dst = ((dkb, rk), (dvb, rv))[t]
        p, slot = nxt(k), 1 if same else 0
        return send(
            src.at[ds(slot * ROWS + p * D, D), :], dst.at[slot, :, ds(hd * D, D)],
            o_s.at[t, slot, k], o_r.at[t, slot, k], dev(x if same else 1 - x, p),
        )

    def backward_part(part, carry):
        wait_in(g_in, g, g_s, g_r, part)
        heads = [part * HEADS + n for n in range(HEADS)]
        run(backward_half(heads, False))

        @pl.when(jnp.logical_and(late, part == SPLIT - 1))
        def _():
            dkb[0:ROWS, :] = (dka[0:ROWS, :] * SCALE).astype(BF16)
            dvb[0:ROWS, :] = dva[0:ROWS, :].astype(BF16)
            for t in range(2):
                for k in range(PEERS):
                    out_copy(t, k, False).start()

        run(backward_half(heads, True))
        return carry

    lax.fori_loop(0, SPLIT, backward_part, 0)

    dkb[ROWS:KEYS, :] = (dka[ROWS:KEYS, :] * SCALE).astype(BF16)
    dvb[ROWS:KEYS, :] = dva[ROWS:KEYS, :].astype(BF16)

    def out_local(t):
        src, dst = ((dkb, rk), (dvb, rv))[t]
        return pltpu.make_async_copy(src.at[ds(ROWS + hd * D, D), :], dst.at[1, :, ds(hd * D, D)], loc.at[t])

    for t in range(2):
        out_local(t).start()
        for k in range(1, PEERS):
            out_copy(t, k, True).start()
    for t in range(2):
        out_local(t).wait()
        for k in range(1, PEERS):
            out_copy(t, k, True).wait()

    @pl.when(late)
    def _():
        for t in range(2):
            for k in range(PEERS):
                out_copy(t, k, False).wait_send()
        dk_out[...] = rk[1]
        dv_out[...] = rv[1]

    @pl.when(x == 0)
    def _():
        for t in range(2):
            for k in range(PEERS):
                out_copy(t, k, False).wait_recv()
                x_copy(t, k).wait_send()
        dk_out[...] = (rk[0].astype(F32) + rk[1].astype(F32)).astype(BF16)
        dv_out[...] = (rv[0].astype(F32) + rv[1].astype(F32)).astype(BF16)

    for t in range(2):
        for k in range(1, PEERS):
            kv_copy(k, t).wait_send()
    for part in range(SPLIT):
        for k in range(1, PEERS):
            in_copy(q_in, q, q_s, q_r, part, k).wait_send()
            in_copy(g_in, g, g_s, g_r, part, k).wait_send()
    for h in range(GROUP):
        dq_local(h).wait()
        for k in range(1, PEERS):
            dq_copy(h, k).wait()


def place(*refs):
    for source, target in zip(refs[:4], refs[4:]):
        target[...] = source[...]


def body(queries, keys, values, cotangent, readout, rewards, saved, ends, segs):
    vmem = pl.BlockSpec(memory_space=pltpu.VMEM)
    hbm = pl.BlockSpec(memory_space=pl.ANY)
    dma = pltpu.SemaphoreType.DMA
    grads = pl.pallas_call(
        kernel,
        out_shape=(
            jax.ShapeDtypeStruct(queries.shape, BF16),
            jax.ShapeDtypeStruct(keys.shape, BF16),
            jax.ShapeDtypeStruct(values.shape, BF16),
            jax.ShapeDtypeStruct((1, D), F32),
        ),
        in_specs=[hbm, hbm, hbm, hbm, vmem, vmem, vmem, vmem, vmem],
        out_specs=(hbm, vmem, vmem, vmem),
        scratch_shapes=[
            pltpu.VMEM((ROWS, ROWS), BF16),
            pltpu.VMEM((ROWS, ROWS), BF16),
            pltpu.VMEM((ROWS, ROWS), BF16),
            pltpu.VMEM((KEYS, 2 * D), BF16),
            pltpu.VMEM((KEYS, D), BF16),
            pltpu.VMEM((D, KEYS), BF16),
            pltpu.VMEM((D, KEYS), BF16),
            pltpu.VMEM((ROWS, D), BF16),
            pltpu.VMEM((GROUP, KEYS, ROWS), BF16),
            pltpu.VMEM((GROUP, D, ROWS), BF16),
            pltpu.VMEM((GROUP, D, ROWS), BF16),
            pltpu.VMEM((KEYS, ROWS), BF16),
            pltpu.VMEM((2, KEYS, T), F32),
            pltpu.VMEM((KEYS, D), F32),
            pltpu.VMEM((KEYS, D), F32),
            pltpu.VMEM((KEYS, D), BF16),
            pltpu.VMEM((KEYS, D), BF16),
            pltpu.VMEM((2, D, ROWS), BF16),
            pltpu.VMEM((2, D, ROWS), BF16),
            pltpu.VMEM((16, 8, D), F32),
            pltpu.VMEM((2, 8, D), F32),
            pltpu.VMEM((PEERS, D), F32),
            pltpu.VMEM((PEERS, PEERS, D), F32),
            pltpu.VMEM((GROUP, PEERS, D), F32),
            pltpu.VMEM((GROUP, D, D), F32),
            pltpu.VMEM((D, D), F32),
            pltpu.VMEM((HEADS, 8, ROWS), F32),
            dma((SPLIT, PEERS)), dma((SPLIT, PEERS)),
            dma((SPLIT, PEERS)), dma((SPLIT, PEERS)),
            dma((GROUP, PEERS)), dma((GROUP, PEERS)),
            dma((2, PEERS)), dma((2, PEERS)),
            dma((2, PEERS)), dma((2, PEERS)),
            dma((16,)), dma((16,)),
            dma, dma,
            dma((PEERS,)), dma((PEERS,)),
            dma((2, 2, PEERS)), dma((2, 2, PEERS)),
            dma((2,)),
        ],
        compiler_params=pltpu.CompilerParams(
            collective_id=0, has_side_effects=True, vmem_limit_bytes=62 << 20
        ),
    )(
        queries, keys, values, cotangent, readout.astype(F32).reshape(1, PEERS * GROUP * D),
        rewards.reshape(1, D), saved.reshape(1, D), ends.reshape(1, D), segs.reshape(1, D),
    )
    blocks = [pl.BlockSpec((D // 2, a.shape[1]), lambda i: (i, 0)) for a in grads[:3]]
    blocks.append(pl.BlockSpec((1, D), lambda i: (0, 0)))
    done = pl.pallas_call(
        place,
        grid=(2,),
        out_shape=[jax.ShapeDtypeStruct(a.shape, a.dtype) for a in grads],
        in_specs=blocks,
        out_specs=blocks,
    )(*grads)
    return (done[0], done[1], done[2], done[3].reshape(D))


def solution(mesh):
    rows, flat = P(("seq", "dp"), None), P(("seq", "dp"))
    return jax.shard_map(
        body,
        mesh=mesh,
        in_specs=(rows, rows, rows, rows, P(), flat, flat, flat, flat),
        out_specs=(rows, rows, rows, flat),
        check_vma=False,
    )
```
